32 devices in a mesh: groups: 2 (over x), replica: 2 (over core), tensor: 8 (over z, y).
Axes of the slice: x: 2, y: 2, z: 4, core: 2. Of those that a mesh axis runs over, the one named last changes fastest.
Arguments:
- activations: bfloat16 [2048, 8192], P(('groups', 'replica'), 'tensor'), parts along dimension 0, may hold values from -800 to 800
- input_norm_scale: float32 [8192], replicated, may hold values from 0.1 to 1.9
- query_weight: bfloat16 [8192, 8192], P(None, 'tensor'), may hold values from -2 to 2
- key_value_weight: bfloat16 [8192, 2048], P('tensor'), may hold values from -1 to 1
- adapter_down_weight: bfloat16 [8192, 4096], P('tensor'), may hold values from -0.0625 to 0.0625
- adapter_up_weight: bfloat16 [4096, 8192], P(None, 'tensor'), may hold values from -1.5 to 1.5
- adapter_index_pairs: int32 [2048, 2], P(('groups', 'replica')), parts along dimension 0, may hold values from 0 to 255, all different within a row
- adapter_mix_weights: float32 [2048, 2], P(('groups', 'replica')), parts along dimension 0, may hold values from 0.25 to 1
- prompt_live_length: int32 [8], P(('groups', 'replica')), parts along dimension 0, may hold values from 64 to 256, as said below
Outputs:
- context: bfloat16 [2048, 8192], P(('groups', 'replica'), 'tensor'), parts along dimension 0
The draws below stay inside these ranges and needn't reach their ends.
There are 2 independent parts, one for each index of `groups`. The reference program is written for one: setup_inputs(seed, part) draws one part's arguments, and reference() takes and returns one part's arrays. A program takes and returns all parts, laid end to end along the dimension named above; an argument that names none is the same for every part. Nothing has to cross between parts.
Inputs may be any that keep to these rules, and one draw needn't show every extreme that they name: `adapter_index_pairs`: the two adapters of a token differ. `prompt_live_length`: some prompt of every draw is live in all 256 positions.
All inputs are finite; a program needn't handle non-finite values.
Results may differ from the reference program's by a relative error of at most 0.0089.
Values may be sent and summed in bfloat16 or wider, within the bound.
No kernel may reach another device: no remote copies, remote signals or barrier semaphores. Data moves between devices by JAX's collectives and lax.ppermute only.
A program may use at most 192 MiB of HBM per device.

```python
import math
import jax
import jax.numpy as jnp
from jax import lax

MODEL_WIDTH = 8192
QUERY_HEADS = 64
KV_HEADS = 8
HEAD_WIDTH = 128
ADAPTER_COUNT = 256
ADAPTER_RANK = 16
SLOT = 256
TOKENS = 1024
PROMPTS = 4


def key_basis(key):
    return jnp.clip(jax.random.normal(jax.random.fold_in(key, 11), (MODEL_WIDTH, KV_HEADS, HEAD_WIDTH)), -6.0, 6.0)


def draw_activations(key, part):
    key = jax.random.fold_in(key, 3)
    key_noise, key_rows, key_cols = jax.random.split(key, 3)
    row_scale = 10.0 ** jax.random.uniform(key_rows, (TOKENS, 1))
    col_scale = 3.0 ** (jnp.arange(MODEL_WIDTH, dtype=jnp.float32)[None, :] / MODEL_WIDTH) * 10.0 ** (0.5 * jax.random.uniform(key_cols, (1, MODEL_WIDTH)))
    noise_base = jnp.clip(jax.random.normal(key_noise, (TOKENS, MODEL_WIDTH)), -6.0, 6.0)
    return (noise_base * row_scale * col_scale).astype(jnp.bfloat16)


def draw_key_value_weight(key, part):
    basis = key_basis(key)
    key = jax.random.fold_in(key, 5)
    value_part = jnp.clip(jax.random.normal(key, (MODEL_WIDTH, KV_HEADS, HEAD_WIDTH)), -6.0, 6.0)
    stacked = jnp.stack([basis, value_part], axis=2) / jnp.sqrt(jnp.float32(MODEL_WIDTH))
    return jnp.clip(stacked, -1.0, 1.0).reshape(MODEL_WIDTH, 2 * KV_HEADS * HEAD_WIDTH).astype(jnp.bfloat16)


def draw_query_weight(key, part):
    key = jax.random.fold_in(key, 7)
    own_part = jnp.clip(jax.random.normal(key, (MODEL_WIDTH, QUERY_HEADS, HEAD_WIDTH)), -6.0, 6.0)
    scaled = own_part / jnp.sqrt(jnp.float32(MODEL_WIDTH))
    return jnp.clip(scaled, -2.0, 2.0).reshape(MODEL_WIDTH, QUERY_HEADS * HEAD_WIDTH).astype(jnp.bfloat16)


def draw_prompt_live_length(key, part):
    key = jax.random.fold_in(key, 9)
    key_lengths, key_full = jax.random.split(key, 2)
    lengths = jax.random.randint(key_lengths, (PROMPTS,), SLOT // 4, SLOT + 1)
    full_index = jax.random.randint(key_full, (), 0, PROMPTS)
    return jnp.where(jnp.arange(PROMPTS) == full_index, SLOT, lengths).astype(jnp.int32)


def levels(key, extent, shards, least, top_value):
    gain = 1.0
    for dim, parts in shards:
        steps = jax.random.uniform(jax.random.fold_in(jax.random.fold_in(key, 6), dim), (parts,), jnp.float32, least / len(shards), top_value / len(shards))
        gain = gain * jnp.repeat(jnp.exp(steps), extent[dim] // parts).reshape((-1,) + (1,) * (len(extent) - 1 - dim))
    return gain


def different_ones(key, rows, amount, top, lift):
    order = jax.random.permutation(jax.random.fold_in(key, 1), amount)
    favour = order
    for power in range(3):
        favour = favour * favour // amount
    favour = favour * lift // amount
    tickets = jax.random.randint(jax.random.fold_in(key, 2), (rows, amount), 0, 4096) + favour
    sure = jax.random.permutation(jax.random.fold_in(key, 3), rows)[jnp.arange(amount) % rows]
    tickets = jnp.where(jnp.arange(rows)[:, None] == sure[None, :], 1 << 14, tickets)
    priority = tickets * amount + jnp.arange(amount)
    return lax.top_k(priority.astype(jnp.int32), top)[1].astype(jnp.int32)


def bell_draw(key, extent, spread, bound, cuts=(), kind=jnp.bfloat16):
    level = levels(key, extent, cuts, -0.22, 0.18) if cuts else 1.0
    result = jax.random.normal(key, extent, jnp.float32) * spread * level
    return jnp.minimum(jnp.maximum(result, -bound), bound).astype(kind)


def setup_inputs(seed: int = 0, part: int = 0) -> dict:
    key_list = jax.random.split(jax.random.key(seed), 10)
    part_keys = jax.random.split(jax.random.fold_in(key_list[9], part), 10)
    return {
        "activations": draw_activations(jax.random.fold_in(jax.random.fold_in(key_list[9], part), 71), part),
        "input_norm_scale": jnp.clip(1.0 + 0.18 * jax.random.normal(key_list[1], (MODEL_WIDTH,), jnp.float32), 0.1, 1.9),
        "query_weight": draw_query_weight(jax.random.fold_in(key_list[9], 71), part),
        "key_value_weight": draw_key_value_weight(jax.random.fold_in(key_list[9], 71), part),
        "adapter_down_weight": bell_draw(key_list[4], (MODEL_WIDTH, ADAPTER_COUNT * ADAPTER_RANK), MODEL_WIDTH ** -0.5, 0.0625, ((0, 8),)),
        "adapter_up_weight": bell_draw(key_list[5], (ADAPTER_COUNT * ADAPTER_RANK, QUERY_HEADS * HEAD_WIDTH), ADAPTER_RANK ** -0.5, 1.5, ((1, 8),)),
        "adapter_index_pairs": different_ones(part_keys[6], TOKENS, ADAPTER_COUNT, 2, 64),
        "adapter_mix_weights": jnp.clip(0.25 + 0.75 * jax.random.uniform(part_keys[7], (TOKENS, 2), jnp.float32) ** levels(part_keys[7], (TOKENS, 2), ((0, 2),), -0.2, 0.2), 0.25, 1.0),
        "prompt_live_length": draw_prompt_live_length(jax.random.fold_in(jax.random.fold_in(key_list[9], part), 71), part),
    }


EPS = 1e-05
ROPE_BASE = 500000.0

def rotate_pairs(values, positions, freq_index, active):
    row_count = values.shape[0]
    pairs = values.reshape(row_count, -1, 2)
    inverse = jnp.power(jnp.float32(ROPE_BASE), -2.0 * freq_index.astype(jnp.float32) / HEAD_WIDTH)
    angles = positions.astype(jnp.float32)[:, None] * inverse[None, :]
    cosine = jnp.where(active[None, :], jnp.cos(angles), 1.0)
    sines = jnp.where(active[None, :], jnp.sin(angles), 0.0)
    first = pairs[:, :, 0]
    second = pairs[:, :, 1]
    turned = jnp.stack([first * cosine - second * sines, first * sines + second * cosine], axis=2)
    return turned.reshape(row_count, -1)

def reference(activations, input_norm_scale, query_weight, key_value_weight, adapter_down_weight, adapter_up_weight, adapter_index_pairs, adapter_mix_weights, prompt_live_length):
    token_count = activations.shape[0]
    values32 = activations.astype(jnp.float32)
    inverse = lax.rsqrt(lax.optimization_barrier(jnp.mean(values32 * values32, axis=1, keepdims=True)) + EPS)
    normalized_input = (values32 * inverse * input_norm_scale[None, :]).astype(jnp.bfloat16)
    positions = jnp.arange(token_count) % SLOT
    q_base = jnp.dot(normalized_input, query_weight, preferred_element_type=jnp.float32)
    kv_raw = jnp.dot(normalized_input, key_value_weight, preferred_element_type=jnp.float32)
    reduced_rank_rows = jnp.dot(normalized_input, adapter_down_weight, preferred_element_type=jnp.float32).reshape(token_count, ADAPTER_COUNT, ADAPTER_RANK)
    onehot = (adapter_index_pairs[:, :, None] == jnp.arange(ADAPTER_COUNT, dtype=jnp.int32)[None, None, :]).astype(jnp.float32)
    low = jnp.einsum('tka,tar->tkr', onehot, reduced_rank_rows, precision=lax.Precision.HIGHEST)
    weighted = low * adapter_mix_weights[:, :, None]
    mixing_factors = jnp.einsum('tka,tkr->tar', onehot, weighted, precision=lax.Precision.HIGHEST)
    mixing_factors = mixing_factors.reshape(token_count, ADAPTER_COUNT * ADAPTER_RANK).astype(jnp.bfloat16)
    query_update = jnp.dot(mixing_factors, adapter_up_weight, preferred_element_type=jnp.float32)
    query_pairs = jnp.arange(QUERY_HEADS * HEAD_WIDTH // 2)
    queries = rotate_pairs(q_base + query_update, positions, 2 * query_pairs % HEAD_WIDTH // 2, query_pairs >= 0).astype(jnp.bfloat16)
    pair_index = jnp.arange(KV_HEADS * HEAD_WIDTH)
    in_head = 2 * pair_index % (2 * HEAD_WIDTH)
    keyvals = rotate_pairs(kv_raw, positions, in_head % HEAD_WIDTH // 2, in_head < HEAD_WIDTH).astype(jnp.bfloat16)
    group_size = QUERY_HEADS // KV_HEADS
    query_blocks = queries.reshape(PROMPTS, SLOT, QUERY_HEADS, HEAD_WIDTH)
    keyval_blocks = keyvals.reshape(PROMPTS, SLOT, KV_HEADS, 2, HEAD_WIDTH)

    def attend(prompt_item):
        query, keyval, length = prompt_item
        key_rows = jnp.repeat(keyval[:, :, 0, :], group_size, axis=1).astype(jnp.float32)
        value_rows = jnp.repeat(keyval[:, :, 1, :], group_size, axis=1).astype(jnp.float32)
        scores = jnp.einsum('shd,uhd->hsu', query.astype(jnp.float32), key_rows, precision=lax.Precision.HIGHEST) / math.sqrt(HEAD_WIDTH)
        row_index = jnp.arange(SLOT)[:, None]
        col_index = jnp.arange(SLOT)[None, :]
        allowed = ((col_index <= row_index) & (col_index < length))[None, :, :]
        masked = jnp.where(allowed, scores, -1e+30)
        row_top = lax.optimization_barrier(jnp.max(masked, axis=2, keepdims=True))
        weights = jnp.where(allowed, jnp.exp(masked - row_top), 0.0)
        totals = lax.optimization_barrier(jnp.sum(weights, axis=2, keepdims=True))
        rounded = lax.optimization_barrier(weights.astype(jnp.bfloat16)).astype(jnp.float32)
        mixed = jnp.einsum('hsu,uhd->shd', rounded, value_rows, precision=lax.Precision.HIGHEST)
        mixed = mixed / jnp.transpose(totals, (1, 0, 2))
        live_rows = (jnp.arange(SLOT) < length)[:, None, None]
        return jnp.where(live_rows, mixed, 0.0).astype(jnp.bfloat16)
    context = lax.map(attend, (query_blocks, keyval_blocks, prompt_live_length))
    return context.reshape(token_count, QUERY_HEADS * HEAD_WIDTH)
```

```python
import functools
import math

import jax
import jax.numpy as jnp
import numpy as np
from jax import lax
from jax.experimental import pallas as pl
from jax.experimental.pallas import tpu as pltpu
from jax.sharding import PartitionSpec as P

QUERY_HEADS = 64
KV_HEADS = 8
HEAD_WIDTH = 128
ADAPTER_RANK = 16
SLOT = 256
LANES = 128
LOW_ROWS = 40

EPS = 1e-05
ROPE_BASE = 500000.0

SIDE_SQUARES = 0
SIDE_MIX = 1
SIDE_INDEX = 3

VMEM_LIMIT = 56 * 1024 * 1024
F32 = jnp.float32
BF16 = jnp.bfloat16


def call(kernel, out_shape, flops, moved, **kwargs):
    return pl.pallas_call(
        kernel,
        out_shape=out_shape,
        compiler_params=pltpu.CompilerParams(vmem_limit_bytes=VMEM_LIMIT),
        cost_estimate=pl.CostEstimate(flops=flops, bytes_accessed=moved, transcendentals=0),
        **kwargs,
    )


def whole(shape):
    return pl.BlockSpec(shape, lambda *_: (0,) * len(shape))


def shape_of(shape, dtype):
    return jax.ShapeDtypeStruct(shape, dtype)


def scale_kernel(pack_ref, x_ref, scale_ref, xs_ref):
    start = pl.multiple_of(pack_ref[0], 16)
    xs_ref[...] = (x_ref[...].astype(F32) * scale_ref[...]).astype(BF16)
    second = (x_ref[SLOT:, :].astype(F32) * scale_ref[...]).astype(BF16)
    xs_ref[pl.ds(start, SLOT), :] = second


def scale_rows(pack, x, scale):
    rows, width = x.shape
    return call(
        scale_kernel,
        shape_of((rows, width), BF16),
        2 * rows * width,
        4 * rows * width,
        grid_spec=pltpu.PrefetchScalarGridSpec(
            num_scalar_prefetch=1,
            grid=(1,),
            in_specs=[whole((rows, width)), whole((1, width))],
            out_specs=whole((rows, width)),
        ),
    )(pack, x, scale)


def side_kernel(pack_ref, x_ref, index_ref, mix_ref, side_ref):
    start = pl.multiple_of(pack_ref[0], 16)
    rows = x_ref.shape[0]
    x = x_ref[...].astype(F32)
    squares = jnp.sum(x * x, axis=1, keepdims=True)
    lane = lax.broadcasted_iota(jnp.int32, (rows, LANES), 1)
    side = jnp.where(lane == SIDE_SQUARES, squares, 0.0)
    for k in range(2):
        side = jnp.where(lane == SIDE_MIX + k, mix_ref[:, k : k + 1], side)
        side = jnp.where(lane == SIDE_INDEX + k, index_ref[:, k : k + 1].astype(F32), side)
    side_ref[...] = side
    side_ref[pl.ds(start, SLOT), :] = side[SLOT:]


def side_rows(pack, x, index, mix):
    rows, width = x.shape
    return call(
        side_kernel,
        shape_of((rows, LANES), F32),
        2 * rows * width,
        2 * rows * width,
        grid_spec=pltpu.PrefetchScalarGridSpec(
            num_scalar_prefetch=1,
            grid=(1,),
            in_specs=[whole((rows, width)), whole((rows, 2)), whole((rows, 2))],
            out_specs=whole((rows, LANES)),
        ),
    )(pack, x, index, mix)


def kv_kernel(xs_ref, w_ref, out_ref):
    out_ref[0] = jnp.dot(xs_ref[...], w_ref[...], preferred_element_type=F32).astype(BF16)


def kv_partials(xs, weight, rows):
    width = xs.shape[1]
    return call(
        kv_kernel,
        shape_of((KV_HEADS, rows, 2 * HEAD_WIDTH), BF16),
        2 * rows * width * weight.shape[1],
        2 * width * weight.shape[1] + 2 * rows * (width + weight.shape[1]),
        grid=(KV_HEADS,),
        in_specs=[
            whole((rows, width)),
            pl.BlockSpec((width, 2 * HEAD_WIDTH), lambda g: (0, g)),
        ],
        out_specs=pl.BlockSpec((1, rows, 2 * HEAD_WIDTH), lambda g: (g, 0, 0)),
    )(xs, weight)


def adapter_of(first, rows):
    lane = lax.broadcasted_iota(jnp.int32, (rows, LANES), 1)
    return ((first + lane) // ADAPTER_RANK).astype(F32)


def low_kernel(rows, xs_ref, w_ref, side_ref, out_ref, acc_ref):
    step = pl.program_id(0)
    tile = w_ref.shape[1]

    @pl.when(step == 0)
    def _():
        acc_ref[...] = jnp.zeros_like(acc_ref)

    product = jnp.dot(xs_ref[...], w_ref[...], preferred_element_type=F32)
    for k in range(2):
        wanted = side_ref[:rows, SIDE_INDEX + k : SIDE_INDEX + k + 1]
        total = acc_ref[k, :rows, :]
        for s in range(tile // LANES):
            adapter = adapter_of(step * tile + s * LANES, 8)[:1]
            total += jnp.where(adapter == wanted, product[:, s * LANES : (s + 1) * LANES], 0.0)
        acc_ref[k, :rows, :] = total

    @pl.when(step == pl.num_programs(0) - 1)
    def _():
        lane = lax.broadcasted_iota(jnp.int32, acc_ref.shape[1:], 1)
        folded = []
        for k in range(2):
            value = acc_ref[k]
            shift = ADAPTER_RANK
            while shift < LANES:
                value = value + pltpu.roll(value, shift, 1)
                shift *= 2
            folded.append(value)
        packed = jnp.where(lane < ADAPTER_RANK, folded[0], folded[1])
        packed = jnp.where(lane < 2 * ADAPTER_RANK, packed, 0.0)
        squares = side_ref[:, SIDE_SQUARES : SIDE_SQUARES + 1]
        packed = jnp.where(lane == 2 * ADAPTER_RANK, squares, packed)
        out_ref[...] = packed.T[:LOW_ROWS]


def low_partials(xs, weight, side, rows):
    width, columns = weight.shape
    tile = min(512, columns)
    tokens = side.shape[0]
    return call(
        functools.partial(low_kernel, rows),
        shape_of((LOW_ROWS, tokens), F32),
        2 * rows * width * columns,
        2 * width * columns,
        grid=(columns // tile,),
        in_specs=[
            whole((rows, width)),
            pl.BlockSpec((width, tile), lambda j: (0, j)),
            whole((tokens, LANES)),
        ],
        out_specs=whole((LOW_ROWS, tokens)),
        scratch_shapes=[pltpu.VMEM((2, tokens, LANES), F32)],
    )(xs, weight, side)


def delta_kernel(rows, model_width, low_ref, side_ref, w_ref, out_ref, inv_ref, co_ref):
    step = pl.program_id(0)
    tile = w_ref.shape[0]

    @pl.when(step == 0)
    def _():
        tokens = low_ref.shape[1]
        padding = jnp.zeros((LANES - LOW_ROWS, tokens), F32)
        low = jnp.concatenate([low_ref[...], padding], axis=0).T
        lane = lax.broadcasted_iota(jnp.int32, (tokens, LANES), 1)
        squares = low[:, 2 * ADAPTER_RANK : 2 * ADAPTER_RANK + 1]
        inverse = lax.rsqrt(squares * (1.0 / model_width) + EPS)
        inv_ref[...] = jnp.broadcast_to(inverse, (tokens, LANES))
        for k in range(2):
            value = jnp.where(lane // ADAPTER_RANK == k, low, 0.0)
            shift = ADAPTER_RANK
            while shift < LANES:
                value = value + pltpu.roll(value, shift, 1)
                shift *= 2
            co_ref[k] = value * inverse * side_ref[:, SIDE_MIX + k : SIDE_MIX + k + 1]
        out_ref[...] = jnp.zeros_like(out_ref)

    wanted = [side_ref[:rows, SIDE_INDEX + k : SIDE_INDEX + k + 1] for k in range(2)]
    pieces = []
    for s in range(tile // LANES):
        adapter = adapter_of(step * tile + s * LANES, 8)[:1]
        piece = jnp.where(adapter == wanted[1], co_ref[1, :rows, :], 0.0)
        piece = jnp.where(adapter == wanted[0], co_ref[0, :rows, :], piece)
        pieces.append(piece.astype(BF16))
    coefficients = jnp.concatenate(pieces, axis=1)
    out_ref[...] += jnp.dot(coefficients, w_ref[...], preferred_element_type=F32)


def query_delta(low, side, weight, rows, model_width):
    depth, columns = weight.shape
    tile = min(512, depth)
    tokens = side.shape[0]
    return call(
        functools.partial(delta_kernel, rows, model_width),
        (shape_of((rows, columns), F32), shape_of((tokens, LANES), F32)),
        2 * rows * depth * columns,
        2 * depth * columns + 4 * rows * columns,
        grid=(depth // tile,),
        in_specs=[
            whole((LOW_ROWS, tokens)),
            whole((tokens, LANES)),
            pl.BlockSpec((tile, columns), lambda j: (j, 0)),
        ],
        out_specs=(whole((rows, columns)), whole((tokens, LANES))),
        scratch_shapes=[pltpu.VMEM((2, tokens, LANES), F32)],
    )(low, side, weight)


def query_kernel(counts, has_total, info_ref, *refs):
    refs = list(refs)
    out_ref = refs.pop()
    total_ref = refs.pop(0) if has_total else None
    weights = refs[-len(counts) :]
    blocks = refs[: -len(counts)]
    start = 0
    for piece in range(counts[0]):
        rows = blocks[piece].shape[0]
        value = total_ref[start : start + rows, :] if has_total else None
        for source, w_ref in enumerate(weights):
            block = blocks[source * counts[0] + piece]
            product = jnp.dot(block[...], w_ref[...], preferred_element_type=F32)
            value = product if value is None else value + product
        out_ref[start : start + rows, :] = value
        start += rows


def query_step(info, total, sources, weight, rows):
    width = weight.shape[0] // info.shape[1]
    columns = weight.shape[1]
    tile = min(512, columns)
    slots = [slot for slot, _ in sources]
    blocks = [block for _, pieces in sources for block in pieces]
    counts = [len(pieces) for _, pieces in sources]
    piece_rows = [rows // counts[0]] * counts[0]
    in_specs = []
    operands = []
    aliases = {}
    if total is not None:
        in_specs.append(pl.BlockSpec((rows, tile), lambda j, _: (0, j)))
        operands.append(total)
        aliases = {1: 0}
    for i, block in enumerate(blocks):
        in_specs.append(whole((piece_rows[i % counts[0]], width)))
        operands.append(block)
    for slot in slots:
        in_specs.append(pl.BlockSpec((width, tile), lambda j, info, slot=slot: (info[0, slot], j)))
        operands.append(weight)
    return call(
        functools.partial(query_kernel, counts, total is not None),
        shape_of((rows, columns), F32),
        2 * rows * width * columns * len(slots),
        2 * width * (columns + rows) * len(slots) + 8 * rows * columns,
        grid_spec=pltpu.PrefetchScalarGridSpec(
            num_scalar_prefetch=1,
            grid=(columns // tile,),
            in_specs=in_specs,
            out_specs=pl.BlockSpec((rows, tile), lambda j, _: (0, j)),
        ),
        input_output_aliases=aliases,
    )(info, *operands)


def rotate(values, cosines, sines):
    lane = lax.broadcasted_iota(jnp.int32, values.shape, 1)
    after = pltpu.roll(values, LANES - 1, 1)
    before = pltpu.roll(values, 1, 1)
    other = jnp.where(lane % 2 == 0, after, before)
    return values * cosines + other * sines


def attention_kernel(
    rows, info_ref, pack_ref, total_ref, delta_ref, inv_ref, first_ref, second_ref, w_ref,
    own_ref, cw_ref, ccw_ref, cos_ref, sin_ref, out_ref, query_s, kv_s, key_s, value_s,
):
    half = rows // 2
    starts = [0, pl.multiple_of(pack_ref[0], 16)]
    lengths = [pack_ref[1], pack_ref[2]]
    inverse = inv_ref[:rows, 0:1]
    row = lax.broadcasted_iota(jnp.int32, (SLOT, SLOT), 0)
    col = lax.broadcasted_iota(jnp.int32, (SLOT, SLOT), 1)
    row_narrow = lax.broadcasted_iota(jnp.int32, (SLOT, HEAD_WIDTH), 0)

    @pl.when(pl.program_id(0) == 0)
    def _():
        raw = own_ref[0].astype(F32) + cw_ref[...].astype(F32) + ccw_ref[...].astype(F32)
        kv_s[:rows, :] = raw * inverse
        kv_s[rows:, :] = jnp.zeros((SLOT, 2 * HEAD_WIDTH), F32)
        query_s[rows:, :] = jnp.zeros((SLOT, query_s.shape[1]), F32)
        for i in range(2):
            pair = kv_s[pl.ds(starts[i], SLOT), :]
            key_s[i] = rotate(pair[:, :HEAD_WIDTH], cos_ref[...], sin_ref[...]).astype(BF16)
            value = jnp.where(row_narrow < lengths[i], pair[:, HEAD_WIDTH:], 0.0)
            value_s[i] = value.astype(BF16)

    for piece, ref in enumerate((first_ref, second_ref)):
        span = slice(piece * half, (piece + 1) * half)
        product = jnp.dot(ref[...], w_ref[...], preferred_element_type=F32)
        query_s[span, :] = (total_ref[span, :] + product) * inverse[span] + delta_ref[span, :]

    for i in range(2):
        allowed = (col <= row) & (col < lengths[i])
        for head in range(w_ref.shape[1] // HEAD_WIDTH):
            span = slice(head * HEAD_WIDTH, (head + 1) * HEAD_WIDTH)
            query = query_s[pl.ds(starts[i], SLOT), span]
            query = rotate(query, cos_ref[...], sin_ref[...]).astype(BF16)
            scores = lax.dot_general(
                query, key_s[i], (((1,), (1,)), ((), ())), preferred_element_type=F32
            ) * (1.0 / math.sqrt(HEAD_WIDTH))
            scores = jnp.where(allowed, scores, -1e30)
            top = jnp.max(scores, axis=1, keepdims=True)
            weights = jnp.where(allowed, jnp.exp(scores - top), 0.0)
            totals = jnp.sum(weights, axis=1, keepdims=True)
            mixed = jnp.dot(weights.astype(BF16), value_s[i], preferred_element_type=F32)
            mixed = jnp.where(row_narrow < lengths[i], mixed / totals, 0.0)
            out_ref[i * SLOT : (i + 1) * SLOT, span] = mixed.astype(BF16)


def attention(info, pack, total, delta, inv, last, last_slot, weight, kv, tables, rows, group_slot):
    width = weight.shape[0] // info.shape[1]
    columns = weight.shape[1]
    tile = min(2 * HEAD_WIDTH, columns)
    own, cw, ccw = kv
    tokens = inv.shape[0]
    pair = 2 * HEAD_WIDTH
    return call(
        functools.partial(attention_kernel, rows),
        shape_of((tokens, columns), BF16),
        2 * rows * width * columns + 4 * tokens * SLOT * columns,
        2 * width * (columns + rows) + 8 * rows * columns + 2 * tokens * columns,
        grid_spec=pltpu.PrefetchScalarGridSpec(
            num_scalar_prefetch=2,
            grid=(columns // tile,),
            in_specs=[
                pl.BlockSpec((rows, tile), lambda j, *_: (0, j)),
                pl.BlockSpec((rows, tile), lambda j, *_: (0, j)),
                whole((tokens, LANES)),
                whole((rows // 2, width)),
                whole((rows // 2, width)),
                pl.BlockSpec((width, tile), lambda j, info, _: (info[0, last_slot], j)),
                pl.BlockSpec((1, rows, pair), lambda j, info, _: (info[1, group_slot], 0, 0)),
                whole((rows, pair)),
                whole((rows, pair)),
                whole((SLOT, HEAD_WIDTH)),
                whole((SLOT, HEAD_WIDTH)),
            ],
            out_specs=pl.BlockSpec((tokens, tile), lambda j, *_: (0, j)),
            scratch_shapes=[
                pltpu.VMEM((rows + SLOT, tile), F32),
                pltpu.VMEM((rows + SLOT, pair), F32),
                pltpu.VMEM((2, SLOT, HEAD_WIDTH), BF16),
                pltpu.VMEM((2, SLOT, HEAD_WIDTH), BF16),
            ],
        ),
    )(info, pack, total, delta, inv, *last, weight, own, cw, ccw, *tables)


def rotation_tables():
    lane = jnp.arange(HEAD_WIDTH)
    inverse = jnp.power(F32(ROPE_BASE), -2.0 * (lane // 2).astype(F32) / HEAD_WIDTH)
    angles = jnp.arange(SLOT).astype(F32)[:, None] * inverse[None, :]
    sines = jnp.sin(angles)
    return jnp.cos(angles), jnp.where(lane[None, :] % 2 == 0, -sines, sines)


def ring_order(count):
    if count > 8:
        return list(range(count))
    return list(range(0, count, 2)) + list(range(1, count, 2))[::-1]


def program(count, rows, pack, info, x, scale, wq, wkv, wdown, wup, index, mix):
    order = ring_order(count)
    half = rows // 2
    reach = count // 2
    cw = [(order[i], order[(i + 1) % count]) for i in range(count)]
    ccw = [(b, a) for a, b in cw]
    send_cw = functools.partial(lax.ppermute, axis_name="tensor", perm=cw)
    send_ccw = functools.partial(lax.ppermute, axis_name="tensor", perm=ccw)
    model_width = wq.shape[0]

    xs = scale_rows(pack, x, scale)
    pieces = [xs[:half], xs[half:rows]]
    side = side_rows(pack, x, index, mix)
    partials = kv_partials(xs, wkv, rows)
    low = low_partials(xs, wdown, side, rows)

    went_cw, went_ccw = list(pieces), list(pieces)
    arrived = []
    for step in range(1, reach):
        for i in range(2):
            went_cw[i] = send_cw(went_cw[i])
            went_ccw[i] = send_ccw(went_ccw[i])
        arrived.append((list(went_cw), list(went_ccw)))
    last = (send_cw(went_cw[0]), send_ccw(went_ccw[1]))

    def block(row):
        return lax.dynamic_index_in_dim(partials, row, 0, keepdims=False)

    def add(a, b):
        return (a.astype(F32) + b.astype(F32)).astype(BF16)

    sums_cw = sums_ccw = None
    for step in range(1, reach + 1):
        own = block(info[1, reach + 1 - step])
        sums_cw = send_cw(own if sums_cw is None else add(sums_cw, own))
        if step < reach:
            own = block(info[1, count - reach + step])
            sums_ccw = send_ccw(own if sums_ccw is None else add(sums_ccw, own))
    if sums_ccw is None:
        sums_ccw = jnp.zeros_like(sums_cw)

    bit = 1
    while bit < count:
        low = low + lax.ppermute(low, "tensor", [(i, i ^ bit) for i in range(count)])
        bit *= 2

    total = query_step(info, None, [(0, [xs])], wq, rows)
    for step in range(1, reach):
        from_cw, from_ccw = arrived[step - 1]
        total = query_step(info, total, [(count - step, from_cw), (step, from_ccw)], wq, rows)
    delta, inv = query_delta(low, side, wup, rows, model_width)
    return attention(
        info, pack, total, delta, inv, last, reach, wq, (partials, sums_cw, sums_ccw),
        rotation_tables(), rows, 0,
    )


def shards(count, x, scale, wq, wkv, wdown, wup, index, mix, lengths):
    width = x.shape[1]
    shard = lax.axis_index("tensor")
    order = ring_order(count)
    group = (wq.shape[1] // HEAD_WIDTH, QUERY_HEADS // KV_HEADS)
    table = np.zeros((count, 2, count), np.int32)
    for place, device in enumerate(order):
        for away in range(count):
            other = order[(place + away) % count]
            table[device, 0, away] = other
            table[device, 1, away] = other * group[0] // group[1]
    info = lax.dynamic_index_in_dim(jnp.asarray(table), shard, 0, keepdims=False)
    scale = lax.dynamic_slice_in_dim(scale, shard * width, width, 0).reshape(1, width)
    live = (lengths + 15) // 16 * 16
    pack = jnp.concatenate([live[:1], lengths])
    rows = x.shape[0]
    return program(count, rows, pack, info, x, scale, wq, wkv, wdown, wup, index, mix)


def solution(mesh):
    placed = (
        P(("groups", "replica"), "tensor"),
        P(),
        P(None, "tensor"),
        P("tensor", None),
        P("tensor", None),
        P(None, "tensor"),
        P(("groups", "replica"), None),
        P(("groups", "replica"), None),
        P(("groups", "replica")),
    )
    return jax.shard_map(
        functools.partial(shards, mesh.shape["tensor"]),
        mesh=mesh,
        in_specs=placed,
        out_specs=P(("groups", "replica"), "tensor"),
        check_vma=False,
    )
```

```python
import functools
import math

import jax
import jax.numpy as jnp
import numpy as np
from jax import lax
from jax.experimental import pallas as pl
from jax.experimental.pallas import tpu as pltpu
from jax.sharding import PartitionSpec as P

QUERY_HEADS = 64
KV_HEADS = 8
HEAD_WIDTH = 128
ADAPTER_RANK = 16
SLOT = 256
LANES = 128
LOW_ROWS = 40

EPS = 1e-05
ROPE_BASE = 500000.0

SIDE_SQUARES = 0
SIDE_MIX = 1
SIDE_INDEX = 3

QUERY_WEIGHT = 8.0
VMEM_LIMIT = 62 * 1024 * 1024
F32 = jnp.float32
BF16 = jnp.bfloat16


def call(kernel, out_shape, microseconds=0.0, **kwargs):
    return pl.pallas_call(
        kernel,
        out_shape=out_shape,
        compiler_params=pltpu.CompilerParams(vmem_limit_bytes=VMEM_LIMIT),
        cost_estimate=pl.CostEstimate(
            flops=int(1.15e9 * microseconds), bytes_accessed=1000, transcendentals=0
        ),
        **kwargs,
    )


def whole(shape):
    return pl.BlockSpec(shape, lambda *_: (0,) * len(shape))


def shape_of(shape, dtype):
    return jax.ShapeDtypeStruct(shape, dtype)


def prefetch(count, grid, in_specs, out_specs, scratch_shapes=()):
    return pltpu.PrefetchScalarGridSpec(
        num_scalar_prefetch=count,
        grid=grid,
        in_specs=in_specs,
        out_specs=out_specs,
        scratch_shapes=scratch_shapes,
    )


def second_start(rows, lengths_ref):
    if rows == 2 * SLOT:
        return SLOT
    return pl.multiple_of((lengths_ref[0] + 15) // 16 * 16, 16)


def write_message(message, block, w_ref):
    half, width = block.shape
    message[:half, :width] = block
    product = jnp.dot(block, w_ref[...], preferred_element_type=F32)
    message[:half, width:] = product.astype(BF16)


def scale_kernel(
    rows, lengths_ref, info_ref, x_ref, scale_ref, cw_w_ref, ccw_w_ref, cw_ref, ccw_ref, packed
):
    packed[...] = (x_ref[...].astype(F32) * scale_ref[...]).astype(BF16)
    if rows != 2 * SLOT:
        packed[pl.ds(second_start(rows, lengths_ref), SLOT), :] = packed[SLOT:, :]
    block = packed[: rows // 2, :]
    write_message(cw_ref, block, cw_w_ref)
    write_message(ccw_ref, block, ccw_w_ref)


def scale_rows(lengths, info, x, scale, weight, rows, reach):
    tokens, width = x.shape
    pair = 2 * HEAD_WIDTH
    message = (rows // 2, width + pair)
    column = [
        pl.BlockSpec((width, pair), lambda j, lengths, info, away=away: (0, info[1, away]))
        for away in (reach, reach + 1)
    ]
    return call(
        functools.partial(scale_kernel, rows),
        (shape_of(message, BF16),) * 2 + (shape_of((tokens, width), BF16),),
        grid_spec=prefetch(
            2,
            (1,),
            [
                whole((tokens, width)),
                pl.BlockSpec((1, width), lambda j, lengths, info: (0, info[0, 0])),
                *column,
            ],
            (whole(message),) * 2 + (whole((tokens, width)),),
        ),
    )(lengths, info, x, scale.reshape(1, -1), weight, weight)


def low_places(tokens, full):
    if full >= 2 * tokens + SLOT:
        second = (slice(0, ADAPTER_RANK), slice(tokens, 2 * tokens))
        squares = (0, slice(2 * tokens, 2 * tokens + SLOT))
        extra = ADAPTER_RANK
    else:
        second = (slice(ADAPTER_RANK, 2 * ADAPTER_RANK), slice(0, tokens))
        squares = (2 * ADAPTER_RANK, slice(0, SLOT))
        extra = 3 * ADAPTER_RANK
    return extra, (slice(0, ADAPTER_RANK), slice(0, tokens)), second, squares


def read_low(region):
    tokens = 2 * SLOT
    _, first, second, (row, lanes) = low_places(tokens, region.shape[1])
    squares = jnp.concatenate(
        [region[row + i : row + i + 1, lanes] + region[row + 2 + i : row + 3 + i, lanes] for i in range(2)],
        axis=1,
    )
    return jnp.concatenate(
        [region[first], region[second], squares, jnp.zeros((LOW_ROWS - 33, tokens), F32)], axis=0
    )


def write_low(message, half, low):
    tokens = 2 * SLOT
    extra, first, second, (row, lanes) = low_places(tokens, message.shape[1])
    message[half : half + extra, :] = jnp.zeros((extra, message.shape[1]), BF16)
    squares = low[2 * ADAPTER_RANK : 2 * ADAPTER_RANK + 1, :]
    rounded = squares.astype(BF16)
    rest = (squares - rounded.astype(F32)).astype(BF16)
    for place, value in ((first, low[:ADAPTER_RANK]), (second, low[ADAPTER_RANK : 2 * ADAPTER_RANK])):
        span = slice(half + place[0].start, half + place[0].stop)
        message[span, place[1]] = value.astype(BF16)
    block = jnp.concatenate(
        [rounded[:, :SLOT], rounded[:, SLOT:], rest[:, :SLOT], rest[:, SLOT:]]
        + [jnp.zeros((ADAPTER_RANK - 4, SLOT), BF16)],
        axis=0,
    )
    message[half + row : half + row + ADAPTER_RANK, lanes] = block


def add_kernel(*refs):
    count = len(refs) // 3
    for i in range(count):
        total = refs[i][...].astype(F32) + refs[count + i][0].astype(F32)
        refs[2 * count + i][...] = total.astype(BF16)


def add_terms(messages, terms, rows):
    half = rows // 2
    full = messages[0].shape[1]
    pair = 2 * HEAD_WIDTH
    lanes = pl.BlockSpec((half, pair), lambda j: (0, full // pair - 1))
    own = [pl.BlockSpec((1, half, pair), lambda j, away=away: (away, 0, 0)) for _, away in terms]
    count = len(messages)
    return call(
        add_kernel,
        (shape_of((half, full), BF16),) * count,
        grid=(1,),
        in_specs=[lanes] * count + own,
        out_specs=(lanes,) * count,
        input_output_aliases={i: i for i in range(count)},
    )(*messages, *[array for array, _ in terms])


def add_low_kernel(half, low_ref, *refs):
    count = len(refs) // 3
    pair = 2 * HEAD_WIDTH
    for i in range(count):
        given, term, out = refs[i], refs[count + i], refs[2 * count + i]
        full = given.shape[1]
        out[:half, : full - pair] = given[:half, : full - pair]
        total = given[:half, full - pair :].astype(F32) + term[0].astype(F32)
        out[:half, full - pair :] = total.astype(BF16)
        write_low(out, half, read_low(given[half:, :].astype(F32)) + low_ref[...])


def add_terms_low(messages, terms, low, rows):
    half = rows // 2
    shape = messages[0].shape
    pair = 2 * HEAD_WIDTH
    own = [pl.BlockSpec((1, half, pair), lambda j, away=away: (away, 1, 0)) for _, away in terms]
    count = len(messages)
    return call(
        functools.partial(add_low_kernel, half),
        (shape_of(shape, BF16),) * count,
        grid=(1,),
        in_specs=[whole(low.shape)] + [whole(shape)] * count + own,
        out_specs=(whole(shape),) * count,
    )(low, *messages, *[array for array, _ in terms])


def kv_kernel(info_ref, x_ref, near_w_ref, far_w_ref, near_ref, far_ref):
    for w_ref, out_ref in ((near_w_ref, near_ref), (far_w_ref, far_ref)):
        product = jnp.dot(x_ref[...], w_ref[...], preferred_element_type=F32)
        out_ref[0] = product.astype(BF16)


def kv_partials(info, packed, weight, rows, count):
    width = weight.shape[0]
    pair = 2 * HEAD_WIDTH
    out = shape_of((count // 2, rows, pair), BF16)
    block = pl.BlockSpec((1, rows, pair), lambda i, info: (i, 0, 0))
    return call(
        kv_kernel,
        (out, out),
        grid_spec=prefetch(
            1,
            (count // 2,),
            [
                whole((rows, width)),
                pl.BlockSpec((width, pair), lambda i, info: (0, info[1, i])),
                pl.BlockSpec((width, pair), lambda i, info: (0, info[1, count // 2 + i])),
            ],
            (block, block),
        ),
    )(info, packed, weight, weight)


def adapter_of(first):
    lane = lax.broadcasted_iota(jnp.int32, (1, LANES), 1)
    return ((first + lane) // ADAPTER_RANK).astype(F32)


def fold(value):
    shift = ADAPTER_RANK
    while shift < LANES:
        value = value + pltpu.roll(value, shift, 1)
        shift *= 2
    return value


def low_kernel(
    rows, lengths_ref, info_ref, x_ref, packed_ref, w_ref, index_ref, mix_ref, cw_w_ref, ccw_w_ref,
    out_ref, side_ref, cw_ref, ccw_ref, acc_ref,
):
    step = pl.program_id(0)
    half = rows // 2
    tile = w_ref.shape[1]
    tokens = x_ref.shape[0]

    @pl.when(step == 0)
    def _():
        acc_ref[...] = jnp.zeros_like(acc_ref)
        x = x_ref[...].astype(F32)
        squares = jnp.sum(x * x, axis=1, keepdims=True)
        given = jnp.concatenate(
            [
                jnp.zeros((1, tokens), F32),
                mix_ref[...],
                index_ref[...].astype(F32),
                jnp.zeros((LANES - 5, tokens), F32),
            ],
            axis=0,
        ).T
        lane = lax.broadcasted_iota(jnp.int32, (tokens, LANES), 1)
        side = jnp.where(lane == SIDE_SQUARES, squares, given)
        side_ref[...] = side
        if rows != tokens:
            side_ref[pl.ds(second_start(rows, lengths_ref), SLOT), :] = side[SLOT:]

    product = jnp.dot(packed_ref[...], w_ref[...], preferred_element_type=F32)
    for k in range(2):
        wanted = side_ref[:rows, SIDE_INDEX + k : SIDE_INDEX + k + 1]
        total = acc_ref[k, :rows, :]
        for s in range(tile // LANES):
            adapter = adapter_of(step * tile + s * LANES)
            part = product[:, s * LANES : (s + 1) * LANES]
            total += jnp.where(adapter == wanted, part, 0.0)
        acc_ref[k, :rows, :] = total

    @pl.when(step == pl.num_programs(0) - 1)
    def _():
        lane = lax.broadcasted_iota(jnp.int32, (tokens, LANES), 1)
        packed = jnp.where(lane < ADAPTER_RANK, fold(acc_ref[0]), fold(acc_ref[1]))
        packed = jnp.where(lane < 2 * ADAPTER_RANK, packed, 0.0)
        squares = side_ref[:, SIDE_SQUARES : SIDE_SQUARES + 1]
        packed = jnp.where(lane == 2 * ADAPTER_RANK, squares, packed)
        low = packed.T[:LOW_ROWS]
        out_ref[...] = low
        for message, w_ref in ((cw_ref, cw_w_ref), (ccw_ref, ccw_w_ref)):
            write_message(message, packed_ref[half:, :], w_ref)
            write_low(message, half, low)


def low_partials(lengths, info, x, packed, weight, index, mix, kv_weight, rows, reach):
    width, columns = weight.shape
    tile = min(1024, columns)
    tokens = x.shape[0]
    pair = 2 * HEAD_WIDTH
    message = (rows // 2 + low_places(tokens, width + pair)[0], width + pair)
    column = [
        pl.BlockSpec((width, pair), lambda j, lengths, info, away=away: (0, info[1, away]))
        for away in (reach - 1, reach)
    ]
    return call(
        functools.partial(low_kernel, rows),
        (shape_of((LOW_ROWS, tokens), F32), shape_of((tokens, LANES), F32))
        + (shape_of(message, BF16),) * 2,
        grid_spec=prefetch(
            2,
            (columns // tile,),
            [
                whole((tokens, width)),
                whole((rows, width)),
                pl.BlockSpec((width, tile), lambda j, *_: (0, j)),
                whole((2, tokens)),
                whole((2, tokens)),
                *column,
            ],
            (whole((LOW_ROWS, tokens)), whole((tokens, LANES)), whole(message), whole(message)),
            [pltpu.VMEM((2, tokens, LANES), F32)],
        ),
    )(lengths, info, x, packed, weight, index.T, mix.T, kv_weight, kv_weight)


def delta_kernel(
    rows, model_width, low_ref, opposite_ref, cw_ref, ccw_ref, side_ref, w_ref, out_ref, inv_ref, co_ref
):
    step = pl.program_id(0)
    tile = w_ref.shape[0]

    @pl.when(step == 0)
    def _():
        tokens = low_ref.shape[1]
        padding = jnp.zeros((LANES - LOW_ROWS, tokens), F32)
        total = low_ref[...] + opposite_ref[...]
        for ref in (cw_ref, ccw_ref):
            total = total + read_low(ref[rows // 2 :, :].astype(F32))
        low = jnp.concatenate([total, padding], axis=0).T
        lane = lax.broadcasted_iota(jnp.int32, (tokens, LANES), 1)
        squares = low[:, 2 * ADAPTER_RANK : 2 * ADAPTER_RANK + 1]
        inverse = lax.rsqrt(squares * (1.0 / model_width) + EPS)
        inv_ref[...] = jnp.broadcast_to(inverse, (tokens, LANES))
        for k in range(2):
            value = fold(jnp.where(lane // ADAPTER_RANK == k, low, 0.0))
            co_ref[k] = value * inverse * side_ref[:, SIDE_MIX + k : SIDE_MIX + k + 1]

    wanted = [side_ref[:rows, SIDE_INDEX + k : SIDE_INDEX + k + 1] for k in range(2)]
    pieces = []
    for s in range(tile // LANES):
        adapter = adapter_of(step * tile + s * LANES)
        piece = jnp.where(adapter == wanted[1], co_ref[1, :rows, :], 0.0)
        piece = jnp.where(adapter == wanted[0], co_ref[0, :rows, :], piece)
        pieces.append(piece.astype(BF16))
    coefficients = jnp.concatenate(pieces, axis=1)
    product = jnp.dot(coefficients, w_ref[...], preferred_element_type=F32)

    @pl.when(step == 0)
    def _():
        out_ref[...] = product

    @pl.when(step > 0)
    def _():
        out_ref[...] += product


def query_delta(lows, messages, side, weight, rows, model_width):
    depth, columns = weight.shape
    tile = min(1024, depth)
    tokens = side.shape[0]
    return call(
        functools.partial(delta_kernel, rows, model_width),
        (shape_of((rows, columns), F32), shape_of((tokens, LANES), F32)),
        grid=(depth // tile,),
        in_specs=[
            whole((LOW_ROWS, tokens)),
            whole((LOW_ROWS, tokens)),
            whole(messages[0].shape),
            whole(messages[1].shape),
            whole((tokens, LANES)),
            pl.BlockSpec((tile, columns), lambda j: (j, 0)),
        ],
        out_specs=(whole((rows, columns)), whole((tokens, LANES))),
        scratch_shapes=[pltpu.VMEM((2, tokens, LANES), F32)],
    )(*lows, *messages, side, weight)


def query_kernel(slots, starts, has_total, info_ref, *refs):
    count = len(slots)
    blocks, weight = refs[:count], refs[count]
    out_ref, x_buf, w_buf, sems, total_sem = refs[-5:]
    half, width = x_buf.shape[1:]

    def copies(i):
        first = pl.multiple_of(info_ref[0, slots[i]] * width, width)
        buf = i % 2
        given = blocks[i].at[pl.ds(starts[i], half), pl.ds(0, width)]
        return [
            pltpu.make_async_copy(given, x_buf.at[buf], sems.at[buf, 0]),
            pltpu.make_async_copy(weight.at[pl.ds(first, width)], w_buf.at[buf], sems.at[buf, 1]),
        ]

    for copy in copies(0):
        copy.start()
    if has_total:
        total_copy = pltpu.make_async_copy(refs[count + 1], out_ref, total_sem)
        total_copy.start()
    for i in range(count):
        if i + 1 < count:
            for copy in copies(i + 1):
                copy.start()
        for copy in copies(i):
            copy.wait()
        product = jnp.dot(x_buf[i % 2], w_buf[i % 2], preferred_element_type=F32)
        if i == 0 and has_total:
            total_copy.wait()
        if i > 0 or has_total:
            out_ref[...] += product
        else:
            out_ref[...] = product


def query_step(info, total, sources, weight, rows):
    half = rows // 2
    columns = weight.shape[1]
    width = weight.shape[0] // info.shape[1]
    operands = [block for _, block, _ in sources] + [weight] + ([] if total is None else [total])
    return call(
        functools.partial(
            query_kernel, [slot for slot, _, _ in sources], [start for _, _, start in sources], total is not None
        ),
        shape_of((half, columns), F32),
        QUERY_WEIGHT,
        grid_spec=prefetch(
            1,
            (1,),
            [pl.BlockSpec(memory_space=pl.ANY)] * len(operands),
            whole((half, columns)),
            [
                pltpu.VMEM((2, half, width), BF16),
                pltpu.VMEM((2, width, columns), BF16),
                pltpu.SemaphoreType.DMA((2, 2)),
                pltpu.SemaphoreType.DMA,
            ],
        ),
    )(info, *operands)


def rotate(values, cosines, sines):
    lane = lax.broadcasted_iota(jnp.int32, values.shape, 1)
    after = pltpu.roll(values, LANES - 1, 1)
    before = pltpu.roll(values, 1, 1)
    other = jnp.where(lane % 2 == 0, after, before)
    return values * cosines + other * sines


def attention_kernel(
    rows, kv_count, info_ref, lengths_ref, total_a_ref, total_b_ref, delta_ref, inv_ref, first_ref,
    second_ref, w_ref, cos_ref, sin_ref, *refs,
):
    kv_refs = refs[:kv_count]
    out_ref, last_s, query_s, kv_s, key_s, value_s, bias_s = refs[kv_count:]
    half = rows // 2
    starts = [0, second_start(rows, lengths_ref)]
    lengths = [lengths_ref[0], lengths_ref[1]]
    inverse = inv_ref[:rows, 0:1]
    row_narrow = lax.broadcasted_iota(jnp.int32, (SLOT, HEAD_WIDTH), 0)

    @pl.when(pl.program_id(0) == 0)
    def _():
        last_s[:half, :] = first_ref[...]
        last_s[half:, :] = second_ref[...]
        for piece in range(2):
            span = slice(piece * half, (piece + 1) * half)
            raw = kv_refs[0][0, span, :].astype(F32)
            for ref in kv_refs[1 + 2 * piece : 3 + 2 * piece]:
                raw = raw + ref[...].astype(F32)
            kv_s[span, :] = raw * inverse[span]
        if rows != 2 * SLOT:
            kv_s[rows:, :] = jnp.zeros((SLOT, 2 * HEAD_WIDTH), F32)
            query_s[rows:, :] = jnp.zeros((SLOT, query_s.shape[1]), F32)
        row = lax.broadcasted_iota(jnp.int32, (SLOT, SLOT), 0)
        col = lax.broadcasted_iota(jnp.int32, (SLOT, SLOT), 1)
        for i in range(2):
            pair = kv_s[pl.ds(starts[i], SLOT), :]
            key_s[i] = rotate(pair[:, :HEAD_WIDTH], cos_ref[...], sin_ref[...]).astype(BF16)
            value = jnp.where(row_narrow < lengths[i], pair[:, HEAD_WIDTH:], 0.0)
            value_s[i] = value.astype(BF16)
            bias_s[i] = jnp.where((col <= row) & (col < lengths[i]), 0.0, -1e30)

    product = jnp.dot(last_s[...], w_ref[...], preferred_element_type=F32)
    for piece, total_ref in enumerate((total_a_ref, total_b_ref)):
        span = slice(piece * half, (piece + 1) * half)
        query_s[span, :] = (total_ref[...] + product[span]) * inverse[span] + delta_ref[span, :]

    factor = math.log2(math.e) / math.sqrt(HEAD_WIDTH)
    for i in range(2):
        for head in range(w_ref.shape[1] // HEAD_WIDTH):
            span = slice(head * HEAD_WIDTH, (head + 1) * HEAD_WIDTH)
            query = query_s[pl.ds(starts[i], SLOT), span]
            query = rotate(query, cos_ref[...], sin_ref[...]).astype(BF16)
            scores = lax.dot_general(
                query, key_s[i], (((1,), (1,)), ((), ())), preferred_element_type=F32
            )
            scores = jnp.where(bias_s[i] == 0.0, scores * factor, -1e30)
            top = jnp.max(scores, axis=1, keepdims=True)
            weights = jnp.exp2(scores - top)
            totals = jnp.sum(weights, axis=1, keepdims=True)
            mixed = jnp.dot(weights.astype(BF16), value_s[i], preferred_element_type=F32)
            mixed = jnp.where(row_narrow < lengths[i], mixed / totals, 0.0)
            out_ref[i * SLOT : (i + 1) * SLOT, span] = mixed.astype(BF16)


def attention(info, lengths, totals, delta, inv, last, last_slot, weight, kv, tables, rows):
    half = rows // 2
    width = weight.shape[0] // info.shape[1]
    columns = weight.shape[1]
    tile = min(2 * HEAD_WIDTH, columns)
    tokens = inv.shape[0]
    pair = 2 * HEAD_WIDTH
    spare = 0 if rows == tokens else SLOT
    return call(
        functools.partial(attention_kernel, rows, len(kv)),
        shape_of((tokens, columns), BF16),
        grid_spec=prefetch(
            2,
            (columns // tile,),
            [
                pl.BlockSpec((half, tile), lambda j, *_: (0, j)),
                pl.BlockSpec((half, tile), lambda j, *_: (0, j)),
                pl.BlockSpec((rows, tile), lambda j, *_: (0, j)),
                whole((tokens, LANES)),
                whole((half, width)),
                whole((half, width)),
                pl.BlockSpec((width, tile), lambda j, info, _: (info[0, last_slot], j)),
                whole((SLOT, HEAD_WIDTH)),
                whole((SLOT, HEAD_WIDTH)),
            ]
            + [pl.BlockSpec((1, rows, pair), lambda j, *_: (0, 0, 0))]
            + [pl.BlockSpec((half, pair), lambda j, *_: (0, width // pair))] * (len(kv) - 1),
            pl.BlockSpec((tokens, tile), lambda j, *_: (0, j)),
            [
                pltpu.VMEM((rows, width), BF16),
                pltpu.VMEM((rows + spare, tile), F32),
                pltpu.VMEM((rows + spare, pair), F32),
                pltpu.VMEM((2, SLOT, HEAD_WIDTH), BF16),
                pltpu.VMEM((2, SLOT, HEAD_WIDTH), BF16),
                pltpu.VMEM((2, SLOT, SLOT), F32),
            ],
        ),
    )(info, lengths, *totals, delta, inv, *last, weight, *tables, *kv)


def rotation_tables():
    lane = jnp.arange(HEAD_WIDTH)
    inverse = jnp.power(F32(ROPE_BASE), -2.0 * (lane // 2).astype(F32) / HEAD_WIDTH)
    angles = jnp.arange(SLOT).astype(F32)[:, None] * inverse[None, :]
    sines = jnp.sin(angles)
    return jnp.cos(angles), jnp.where(lane[None, :] % 2 == 0, -sines, sines)


def ring_order(count):
    if count > 8:
        return list(range(count))
    return list(range(0, count, 2)) + list(range(1, count, 2))[::-1]


def after(value, *earlier):
    return lax.optimization_barrier((value, *earlier))[0]


def program(count, rows, lengths, info, x, scale, wq, wkv, wdown, wup, index, mix):
    order = ring_order(count)
    reach = count // 2
    cw = [(order[i], order[(i + 1) % count]) for i in range(count)]
    ccw = [(b, a) for a, b in cw]
    send_cw = functools.partial(lax.ppermute, axis_name="tensor", perm=cw)
    send_ccw = functools.partial(lax.ppermute, axis_name="tensor", perm=ccw)

    opposite = [(order[i], order[(i + reach) % count]) for i in range(count)]

    cw_first, ccw_first, packed = scale_rows(lengths, info, x, scale, wkv, rows, reach)
    from_cw, from_ccw = [send_cw(cw_first), None], [send_ccw(ccw_first), None]
    low, side, cw_second, ccw_second = low_partials(
        lengths, info, x, packed, wdown, index, mix, wkv, rows, reach
    )
    from_cw[1], from_ccw[1] = send_cw(cw_second), send_ccw(ccw_second)
    low_opposite = lax.ppermute(low, "tensor", opposite)
    near, far = kv_partials(info, after(packed, low), wkv, rows, count)
    done = near
    totals = [None, None]
    delta = inv = None

    def term(away):
        return (near, away) if away < reach else (far, away - reach)

    for step in range(1, reach):
        final = step + 1 == reach
        for piece in range(2):
            got_cw, got_ccw, _ = lax.optimization_barrier((from_cw[piece], from_ccw[piece], done))
            ahead = term(reach - step - piece)
            behind = term(count - reach + step + 1 - piece)
            if final and piece == 1:
                late, _ = lax.optimization_barrier((low_opposite, got_cw))
                delta, inv = query_delta(
                    (low, late), (got_cw, got_ccw), side, wup, rows, wq.shape[0]
                )
            if not final:
                if piece == 0:
                    got_cw, got_ccw = add_terms([got_cw, got_ccw], [ahead, behind], rows)
                else:
                    got_cw, got_ccw = add_terms_low([got_cw, got_ccw], [ahead, behind], low, rows)
                from_cw[piece], from_ccw[piece] = send_cw(got_cw), send_ccw(got_ccw)
            elif piece == 0:
                (got_cw,) = add_terms([got_cw], [ahead], rows)
                from_cw[0], from_ccw[0] = send_cw(got_cw), got_ccw
            else:
                (got_ccw,) = add_terms_low([got_ccw], [behind], low, rows)
                from_cw[1], from_ccw[1] = got_cw, send_ccw(got_ccw)
            sources = [(count - step, got_cw, 0), (step, got_ccw, 0)]
            if step == 1:
                sources = [(0, packed, piece * (rows // 2))] + sources
            totals[piece] = query_step(info, totals[piece], sources, wq, rows)
            done = totals[piece]
    kv = (near, from_cw[0], from_ccw[0], from_cw[1], from_ccw[1])
    return attention(
        info, lengths, totals, delta, inv, (from_cw[0], from_ccw[1]), reach, wq, kv,
        rotation_tables(), rows,
    )


def shards(count, x, scale, wq, wkv, wdown, wup, index, mix, lengths):
    shard = lax.axis_index("tensor")
    order = ring_order(count)
    heads = wq.shape[1] // HEAD_WIDTH
    table = np.zeros((count, 2, count), np.int32)
    for place, device in enumerate(order):
        for i in range(count):
            other = order[(place + i) % count]
            table[device, 0, i] = other
            table[device, 1, i] = other * heads // (QUERY_HEADS // KV_HEADS)
    info = lax.dynamic_index_in_dim(jnp.asarray(table), shard, 0, keepdims=False)
    return program(count, x.shape[0], lengths, info, x, scale, wq, wkv, wdown, wup, index, mix)


def solution(mesh):
    placed = (
        P(("groups", "replica"), "tensor"),
        P(),
        P(None, "tensor"),
        P("tensor", None),
        P("tensor", None),
        P(None, "tensor"),
        P(("groups", "replica"), None),
        P(("groups", "replica"), None),
        P(("groups", "replica")),
    )
    return jax.shard_map(
        functools.partial(shards, mesh.shape["tensor"]),
        mesh=mesh,
        in_specs=placed,
        out_specs=P(("groups", "replica"), "tensor"),
        check_vma=False,
    )
```

```python
import functools
import math

import jax
import jax.numpy as jnp
import numpy as np
from jax import lax
from jax.experimental import pallas as pl
from jax.experimental.pallas import tpu as pltpu
from jax.sharding import PartitionSpec as P

QUERY_HEADS = 64
KV_HEADS = 8
HEAD_WIDTH = 128
ADAPTER_RANK = 16
SLOT = 256
LANES = 128
LOW_ROWS = 40

EPS = 1e-05
ROPE_BASE = 500000.0

SIDE_SQUARES = 0
SIDE_MIX = 1
SIDE_INDEX = 3

DEPTH = 3
CHUNK = 512
HEADS_AT_ONCE = 8
DELTA_TILE = 1024
ADD_WEIGHT = 8.0
QUERY_WEIGHT = 8.0
VMEM_LIMIT = 64 * 1024 * 1024 - 64 * 1024
F32 = jnp.float32
BF16 = jnp.bfloat16


def call(kernel, out_shape, microseconds=0.0, **kwargs):
    return pl.pallas_call(
        kernel,
        out_shape=out_shape,
        compiler_params=pltpu.CompilerParams(vmem_limit_bytes=VMEM_LIMIT),
        cost_estimate=pl.CostEstimate(
            flops=int(1.15e9 * microseconds), bytes_accessed=1000, transcendentals=0
        ),
        **kwargs,
    )


def whole(shape):
    return pl.BlockSpec(shape, lambda *_: (0,) * len(shape))


def shape_of(shape, dtype):
    return jax.ShapeDtypeStruct(shape, dtype)


def prefetch(count, grid, in_specs, out_specs, scratch_shapes=()):
    return pltpu.PrefetchScalarGridSpec(
        num_scalar_prefetch=count,
        grid=grid,
        in_specs=in_specs,
        out_specs=out_specs,
        scratch_shapes=scratch_shapes,
    )


def second_start(rows, lengths_ref):
    if rows == 2 * SLOT:
        return SLOT
    return pl.multiple_of((lengths_ref[0] + 15) // 16 * 16, 16)


def write_message(message, block, w_ref):
    half, width = block.shape
    message[:half, :width] = block
    product = jnp.dot(block, w_ref[...], preferred_element_type=F32)
    message[:half, width:] = product.astype(BF16)


def scale_kernel(
    rows, lengths_ref, info_ref, x_ref, scale_ref, cw_w_ref, ccw_w_ref, cw_ref, ccw_ref, packed
):
    packed[...] = (x_ref[...].astype(F32) * scale_ref[...]).astype(BF16)
    if rows != 2 * SLOT:
        packed[pl.ds(second_start(rows, lengths_ref), SLOT), :] = packed[SLOT:, :]
    block = packed[: rows // 2, :]
    write_message(cw_ref, block, cw_w_ref)
    write_message(ccw_ref, block, ccw_w_ref)


def scale_rows(lengths, info, x, scale, weight, rows, reach):
    tokens, width = x.shape
    pair = 2 * HEAD_WIDTH
    message = (rows // 2, width + pair)
    column = [
        pl.BlockSpec((width, pair), lambda j, lengths, info, away=away: (0, info[1, away]))
        for away in (reach, reach + 1)
    ]
    return call(
        functools.partial(scale_kernel, rows),
        (shape_of(message, BF16),) * 2 + (shape_of((tokens, width), BF16),),
        grid_spec=prefetch(
            2,
            (1,),
            [
                whole((tokens, width)),
                pl.BlockSpec((1, width), lambda j, lengths, info: (0, info[0, 0])),
                *column,
            ],
            (whole(message),) * 2 + (whole((tokens, width)),),
        ),
    )(lengths, info, x, scale.reshape(1, -1), weight, weight)


def low_places(tokens, full):
    if full >= 2 * tokens + SLOT:
        second = (slice(0, ADAPTER_RANK), slice(tokens, 2 * tokens))
        squares = (0, slice(2 * tokens, 2 * tokens + SLOT))
        extra = ADAPTER_RANK
    else:
        second = (slice(ADAPTER_RANK, 2 * ADAPTER_RANK), slice(0, tokens))
        squares = (2 * ADAPTER_RANK, slice(0, SLOT))
        extra = 3 * ADAPTER_RANK
    return extra, (slice(0, ADAPTER_RANK), slice(0, tokens)), second, squares


def read_low(region):
    tokens = 2 * SLOT
    _, first, second, (row, lanes) = low_places(tokens, region.shape[1])
    squares = jnp.concatenate(
        [region[row + i : row + i + 1, lanes] + region[row + 2 + i : row + 3 + i, lanes] for i in range(2)],
        axis=1,
    )
    return jnp.concatenate(
        [region[first], region[second], squares, jnp.zeros((LOW_ROWS - 33, tokens), F32)], axis=0
    )


def write_low(message, half, low):
    tokens = 2 * SLOT
    extra, first, second, (row, lanes) = low_places(tokens, message.shape[1])
    message[half : half + extra, :] = jnp.zeros((extra, message.shape[1]), BF16)
    squares = low[2 * ADAPTER_RANK : 2 * ADAPTER_RANK + 1, :]
    rounded = squares.astype(BF16)
    rest = (squares - rounded.astype(F32)).astype(BF16)
    for place, value in ((first, low[:ADAPTER_RANK]), (second, low[ADAPTER_RANK : 2 * ADAPTER_RANK])):
        span = slice(half + place[0].start, half + place[0].stop)
        message[span, place[1]] = value.astype(BF16)
    block = jnp.concatenate(
        [rounded[:, :SLOT], rounded[:, SLOT:], rest[:, :SLOT], rest[:, SLOT:]]
        + [jnp.zeros((ADAPTER_RANK - 4, SLOT), BF16)],
        axis=0,
    )
    message[half + row : half + row + ADAPTER_RANK, lanes] = block


def add_kernel(info_ref, block_ref, *refs):
    count = len(refs) // 3
    for i in range(count):
        own = jnp.dot(block_ref[...], refs[count + i][...], preferred_element_type=F32)
        refs[2 * count + i][...] = (refs[i][...].astype(F32) + own).astype(BF16)


def add_terms(info, messages, aways, packed, weight, rows):
    half = rows // 2
    width = weight.shape[0]
    full = messages[0].shape[1]
    pair = 2 * HEAD_WIDTH
    lanes = pl.BlockSpec((half, pair), lambda j, info: (0, full // pair - 1))
    columns = [
        pl.BlockSpec((width, pair), lambda j, info, away=away: (0, info[1, away]))
        for away in aways
    ]
    count = len(messages)
    return call(
        add_kernel,
        (shape_of((half, full), BF16),) * count,
        ADD_WEIGHT,
        grid_spec=prefetch(
            1,
            (1,),
            [pl.BlockSpec((half, width), lambda j, info: (0, 0))] + [lanes] * count + columns,
            (lanes,) * count,
        ),
        input_output_aliases={2 + i: i for i in range(count)},
    )(info, packed, *messages, *[weight] * count)


def add_low_kernel(half, info_ref, block_ref, low_ref, *refs):
    count = len(refs) // 3
    pair = 2 * HEAD_WIDTH
    around = low_ref[...]
    for i in range(count):
        given, w_ref, out = refs[i], refs[count + i], refs[2 * count + i]
        full = given.shape[1]
        out[:half, : full - pair] = given[:half, : full - pair]
        own = jnp.dot(block_ref[...], w_ref[...], preferred_element_type=F32)
        out[:half, full - pair :] = (given[:half, full - pair :].astype(F32) + own).astype(BF16)
        sums = read_low(given[half:, :].astype(F32))
        around = around + sums
        write_low(out, half, sums + low_ref[...])
    refs[3 * count][...] = around


def add_terms_low(info, messages, aways, packed, weight, low, rows):
    half = rows // 2
    width = weight.shape[0]
    shape = messages[0].shape
    pair = 2 * HEAD_WIDTH
    columns = [
        pl.BlockSpec((width, pair), lambda j, info, away=away: (0, info[1, away]))
        for away in aways
    ]
    count = len(messages)
    return call(
        functools.partial(add_low_kernel, half),
        (shape_of(shape, BF16),) * count + (shape_of(low.shape, F32),),
        ADD_WEIGHT,
        grid_spec=prefetch(
            1,
            (1,),
            [pl.BlockSpec((half, width), lambda j, info: (1, 0)), whole(low.shape)]
            + [whole(shape)] * count
            + columns,
            (whole(shape),) * count + (whole(low.shape),),
        ),
    )(info, packed, low, *messages, *[weight] * count)


def chosen_group(index):
    rows = index.shape[0]
    lane = lax.broadcasted_iota(jnp.int32, (rows, LANES), 1)
    return index - (lane // ADAPTER_RANK).astype(F32)


def fold(value):
    shift = ADAPTER_RANK
    while shift < LANES:
        value = value + pltpu.roll(value, shift, 1)
        shift *= 2
    return value


def low_kernel(
    rows, lengths_ref, info_ref, x_ref, packed_ref, w_ref, index_ref, mix_ref, cw_w_ref, ccw_w_ref,
    own_w_ref, out_ref, side_ref, cw_ref, ccw_ref, own_ref, acc_ref, group_ref,
):
    step = pl.program_id(0)
    half = rows // 2
    tile = w_ref.shape[1]
    tokens = x_ref.shape[0]

    @pl.when(step == 0)
    def _():
        acc_ref[...] = jnp.zeros_like(acc_ref)
        x = x_ref[...].astype(F32)
        squares = jnp.sum(x * x, axis=1, keepdims=True)
        given = jnp.concatenate(
            [
                jnp.zeros((1, tokens), F32),
                mix_ref[...],
                index_ref[...].astype(F32),
                jnp.zeros((LANES - 5, tokens), F32),
            ],
            axis=0,
        ).T
        lane = lax.broadcasted_iota(jnp.int32, (tokens, LANES), 1)
        side = jnp.where(lane == SIDE_SQUARES, squares, given)
        side_ref[...] = side
        if rows != tokens:
            side_ref[pl.ds(second_start(rows, lengths_ref), SLOT), :] = side[SLOT:]
        for k in range(2):
            group_ref[k] = chosen_group(side_ref[:, SIDE_INDEX + k : SIDE_INDEX + k + 1])

    chunk = min(CHUNK, tile)

    def part(n, carry):
        first = pl.multiple_of(n * chunk, chunk)
        product = jnp.dot(
            packed_ref[...], w_ref[:, pl.ds(first, chunk)], preferred_element_type=F32
        )
        for k in range(2):
            total = acc_ref[k, :rows, :]
            for s in range(chunk // LANES):
                group = (step * tile + first + s * LANES) // ADAPTER_RANK
                here = group_ref[k, :rows, :] == group.astype(F32)
                total += jnp.where(here, product[:, s * LANES : (s + 1) * LANES], 0.0)
            acc_ref[k, :rows, :] = total
        return carry

    lax.fori_loop(0, tile // chunk, part, 0)

    @pl.when(step == pl.num_programs(0) - 1)
    def _():
        lane = lax.broadcasted_iota(jnp.int32, (tokens, LANES), 1)
        packed = jnp.where(lane < ADAPTER_RANK, fold(acc_ref[0]), fold(acc_ref[1]))
        packed = jnp.where(lane < 2 * ADAPTER_RANK, packed, 0.0)
        squares = side_ref[:, SIDE_SQUARES : SIDE_SQUARES + 1]
        packed = jnp.where(lane == 2 * ADAPTER_RANK, squares, packed)
        low = packed.T[:LOW_ROWS]
        out_ref[...] = low
        for message, w_ref in ((cw_ref, cw_w_ref), (ccw_ref, ccw_w_ref)):
            write_message(message, packed_ref[half:, :], w_ref)
            write_low(message, half, low)
        own = jnp.dot(packed_ref[...], own_w_ref[...], preferred_element_type=F32)
        own_ref[...] = own.astype(BF16)


def low_partials(lengths, info, x, packed, weight, index, mix, kv_weight, rows, reach):
    width, columns = weight.shape
    tile = min(1024, columns)
    tokens = x.shape[0]
    pair = 2 * HEAD_WIDTH
    message = (rows // 2 + low_places(tokens, width + pair)[0], width + pair)
    column = [
        pl.BlockSpec((width, pair), lambda j, lengths, info, away=away: (0, info[1, away]))
        for away in (reach - 1, reach, 0)
    ]
    return call(
        functools.partial(low_kernel, rows),
        (shape_of((LOW_ROWS, tokens), F32), shape_of((tokens, LANES), F32))
        + (shape_of(message, BF16),) * 2
        + (shape_of((rows, pair), BF16),),
        grid_spec=prefetch(
            2,
            (columns // tile,),
            [
                whole((tokens, width)),
                whole((rows, width)),
                pl.BlockSpec((width, tile), lambda j, *_: (0, j)),
                whole((2, tokens)),
                whole((2, tokens)),
                *column,
            ],
            (whole((LOW_ROWS, tokens)), whole((tokens, LANES)), whole(message), whole(message))
            + (whole((rows, pair)),),
            [pltpu.VMEM((2, tokens, LANES), F32)] * 2,
        ),
    )(lengths, info, x, packed, weight, index.T, mix.T, kv_weight, kv_weight, kv_weight)


def delta_kernel(
    half, model_width, low_ref, opposite_ref, cw_ref, ccw_ref, side_ref, w_ref, out_ref, inv_ref,
    co_ref, group_ref, ends, sems,
):
    step = pl.program_id(0)
    tile = w_ref.shape[0]

    @pl.when(step == 0)
    def _():
        copies = [
            pltpu.make_async_copy(ref.at[pl.ds(half, ends.shape[1])], ends.at[i], sems.at[i])
            for i, ref in enumerate((cw_ref, ccw_ref))
        ]
        for copy in copies:
            copy.start()
        for k in range(2):
            group_ref[k] = chosen_group(side_ref[:, SIDE_INDEX + k : SIDE_INDEX + k + 1])
        for copy in copies:
            copy.wait()
        tokens = low_ref.shape[1]
        sums = low_ref[...] + opposite_ref[...]
        for i in range(2):
            sums = sums + read_low(ends[i].astype(F32))
        padding = jnp.zeros((LANES - LOW_ROWS, tokens), F32)
        low = jnp.concatenate([sums, padding], axis=0).T
        lane = lax.broadcasted_iota(jnp.int32, (tokens, LANES), 1)
        squares = low[:, 2 * ADAPTER_RANK : 2 * ADAPTER_RANK + 1]
        inverse = lax.rsqrt(squares * (1.0 / model_width) + EPS)
        inv_ref[...] = jnp.broadcast_to(inverse, (tokens, LANES))
        for k in range(2):
            value = fold(jnp.where(lane // ADAPTER_RANK == k, low, 0.0))
            co_ref[k] = value * inverse * side_ref[:, SIDE_MIX + k : SIDE_MIX + k + 1]
        out_ref[...] = jnp.zeros_like(out_ref)

    pieces = []
    for s in range(tile // LANES):
        group = ((step * tile + s * LANES) // ADAPTER_RANK).astype(F32)
        piece = jnp.where(group_ref[0] == group, co_ref[0], 0.0)
        piece = jnp.where(group_ref[1] == group, co_ref[1], piece)
        pieces.append(piece.astype(BF16))
    coefficients = jnp.concatenate(pieces, axis=1)
    out_ref[...] += jnp.dot(coefficients, w_ref[...], preferred_element_type=F32)


def query_delta(low, opposite, cw, ccw, side, weight, model_width):
    depth, columns = weight.shape
    tile = min(DELTA_TILE, depth)
    tokens = side.shape[0]
    anywhere = pl.BlockSpec(memory_space=pl.ANY)
    extra = low_places(tokens, cw.shape[1])[0]
    return call(
        functools.partial(delta_kernel, tokens // 2, model_width),
        (shape_of((tokens, columns), F32), shape_of((tokens, LANES), F32)),
        QUERY_WEIGHT,
        grid=(depth // tile,),
        in_specs=[whole(low.shape), whole(low.shape), anywhere, anywhere, whole(side.shape)]
        + [pl.BlockSpec((tile, columns), lambda j: (j, 0))],
        out_specs=(whole((tokens, columns)), whole((tokens, LANES))),
        scratch_shapes=[
            pltpu.VMEM((2, tokens, LANES), F32),
            pltpu.VMEM((2, tokens, LANES), F32),
            pltpu.VMEM((2, extra, cw.shape[1]), BF16),
            pltpu.SemaphoreType.DMA((2,)),
        ],
    )(low, opposite, cw, ccw, side, weight)


def product_kernel(slots, starts, has_total, place, info_ref, *refs):
    refs = list(refs)
    count = len(slots)
    blocks = [refs.pop(0) for _ in range(count)]
    weight = refs.pop(0)
    total_ref = refs.pop(0) if has_total else None
    delta_ref, inv_ref = (None, None) if place is None else (refs.pop(0), refs.pop(0))
    out_ref, x_buf, w_buf, sems, total_sems, *refs = refs
    depth, half, width = x_buf.shape
    columns = w_buf.shape[2]
    chunk = min(CHUNK, columns)

    def copies(i):
        buf = i % depth
        first = pl.multiple_of(info_ref[0, slots[i]] * width, width)
        block = blocks[i].at[pl.ds(starts[i], half), pl.ds(0, width)]
        return [
            pltpu.make_async_copy(weight.at[pl.ds(first, width)], w_buf.at[buf], sems.at[buf, 0]),
            pltpu.make_async_copy(block, x_buf.at[buf], sems.at[buf, 1]),
        ]

    for i in range(min(depth - 1, count)):
        for copy in copies(i):
            copy.start()
    if has_total:
        total_copy = pltpu.make_async_copy(total_ref, out_ref, total_sems.at[0])
        total_copy.start()
    if place is not None:
        given = delta_ref.at[pl.ds(place * half, half)]
        delta_copy = pltpu.make_async_copy(given, refs[0], total_sems.at[1])
        delta_copy.start()
    for i in range(count):
        buf = i % depth
        if i + depth - 1 < count:
            for copy in copies(i + depth - 1):
                copy.start()
        for copy in copies(i):
            copy.wait()
        if i == 0 and has_total:
            total_copy.wait()
        if i == count - 1 and place is not None:
            delta_copy.wait()
        for first in range(0, columns, chunk):
            span = slice(first, first + chunk)
            value = jnp.dot(x_buf[buf], w_buf[buf, :, span], preferred_element_type=F32)
            if i > 0 or has_total:
                value = out_ref[:, span] + value
            if i == count - 1 and place is not None:
                value = value * inv_ref[:, 0:1] + refs[0][:, span]
            out_ref[:, span] = value


def product(info, total, sources, weight, half, ending=None, place=None):
    columns = weight.shape[1]
    width = weight.shape[0] // info.shape[1]
    operands = [block for _, block, _ in sources]
    operands += [weight] + ([] if total is None else [total])
    in_specs = [pl.BlockSpec(memory_space=pl.ANY)] * len(operands)
    scratch = [
        pltpu.VMEM((DEPTH, half, width), BF16),
        pltpu.VMEM((DEPTH, width, columns), BF16),
        pltpu.SemaphoreType.DMA((DEPTH, 2)),
        pltpu.SemaphoreType.DMA((2,)),
    ]
    if ending is not None:
        operands += ending
        in_specs += [pl.BlockSpec(memory_space=pl.ANY)]
        in_specs += [pl.BlockSpec((half, LANES), lambda j, info: (place, 0))]
        scratch += [pltpu.VMEM((half, columns), F32)]
    slots = [slot for slot, _, _ in sources]
    starts = [start for _, _, start in sources]
    return call(
        functools.partial(product_kernel, slots, starts, total is not None, place),
        shape_of((half, columns), F32),
        QUERY_WEIGHT,
        grid_spec=prefetch(1, (1,), in_specs, whole((half, columns)), scratch),
    )(info, *operands)


def rotate(values, cosines, sines):
    lane = lax.broadcasted_iota(jnp.int32, values.shape, 1)
    after = pltpu.roll(values, LANES - 1, 1)
    before = pltpu.roll(values, 1, 1)
    other = jnp.where(lane % 2 == 0, after, before)
    return values * cosines + other * sines


def attention_kernel(
    prompt, info_ref, lengths_ref, total_ref, inv_ref, last_ref, w_ref, cos_ref, sin_ref, own_ref,
    cw_ref, ccw_ref, out_ref, key_s, value_s, bias_s,
):
    length = lengths_ref[prompt]
    inverse = inv_ref[:, 0:1]
    row_narrow = lax.broadcasted_iota(jnp.int32, (SLOT, HEAD_WIDTH), 0)

    @pl.when(pl.program_id(0) == 0)
    def _():
        pair = own_ref[...].astype(F32) + cw_ref[...].astype(F32) + ccw_ref[...].astype(F32)
        pair = pair * inverse
        key_s[...] = rotate(pair[:, :HEAD_WIDTH], cos_ref[...], sin_ref[...]).astype(BF16)
        value_s[...] = pair[:, HEAD_WIDTH:].astype(BF16)
        row = lax.broadcasted_iota(jnp.int32, (SLOT, SLOT), 0)
        col = lax.broadcasted_iota(jnp.int32, (SLOT, SLOT), 1)
        bias_s[...] = jnp.where((col <= row) & (col < length), 0.0, -1e30)

    product = jnp.dot(last_ref[...], w_ref[...], preferred_element_type=F32)
    queries = total_ref[...] + product * inverse
    factor = math.log2(math.e) / math.sqrt(HEAD_WIDTH)
    for head in range(w_ref.shape[1] // HEAD_WIDTH):
        span = slice(head * HEAD_WIDTH, (head + 1) * HEAD_WIDTH)
        query = rotate(queries[:, span], cos_ref[...], sin_ref[...]).astype(BF16)
        scores = lax.dot_general(
            query, key_s[...], (((1,), (1,)), ((), ())), preferred_element_type=F32
        )
        scores = scores * factor + bias_s[...]
        top = jnp.max(scores, axis=1, keepdims=True)
        weights = jnp.exp2(scores - top)
        totals = jnp.sum(weights, axis=1, keepdims=True)
        mixed = jnp.dot(weights.astype(BF16), value_s[...], preferred_element_type=F32)
        mixed = jnp.where(row_narrow < length, mixed * (1.0 / totals), 0.0)
        out_ref[:, span] = mixed.astype(BF16)


def attention(info, lengths, total, inv, last, last_slot, weight, kv, tables, prompt, done=None):
    width = weight.shape[0] // info.shape[1]
    columns = weight.shape[1]
    tile = min(HEADS_AT_ONCE * HEAD_WIDTH, columns)
    pair = 2 * HEAD_WIDTH
    own, cw, ccw = kv
    kernel = functools.partial(attention_kernel, prompt)
    operands = [total, inv, last, weight, *tables, own, cw, ccw]
    in_specs = [
        pl.BlockSpec((SLOT, tile), lambda j, *_: (0, j)),
        pl.BlockSpec((SLOT, LANES), lambda j, *_: (prompt, 0)),
        pl.BlockSpec((SLOT, width), lambda j, *_: (0, 0)),
        pl.BlockSpec((width, tile), lambda j, info, _: (info[0, last_slot], j)),
        whole((SLOT, HEAD_WIDTH)),
        whole((SLOT, HEAD_WIDTH)),
        pl.BlockSpec((SLOT, pair), lambda j, *_: (prompt, 0)),
        pl.BlockSpec((SLOT, pair), lambda j, *_: (0, width // pair)),
        pl.BlockSpec((SLOT, pair), lambda j, *_: (0, width // pair)),
    ]
    aliases = {}
    if done is not None:
        inner = kernel

        def kernel(*refs):
            return inner(*refs[:11], *refs[12:])

        operands.append(done)
        in_specs.append(pl.BlockSpec(memory_space=pl.ANY))
        aliases = {11: 0}
    return call(
        kernel,
        shape_of((2 * SLOT, columns), BF16),
        grid_spec=prefetch(
            2,
            (columns // tile,),
            in_specs,
            pl.BlockSpec((SLOT, tile), lambda j, *_: (prompt, j)),
            [
                pltpu.VMEM((SLOT, HEAD_WIDTH), BF16),
                pltpu.VMEM((SLOT, HEAD_WIDTH), BF16),
                pltpu.VMEM((SLOT, SLOT), F32),
            ],
        ),
        input_output_aliases=aliases,
    )(info, lengths, *operands)


def rotation_tables():
    lane = jnp.arange(HEAD_WIDTH)
    inverse = jnp.power(F32(ROPE_BASE), -2.0 * (lane // 2).astype(F32) / HEAD_WIDTH)
    angles = jnp.arange(SLOT).astype(F32)[:, None] * inverse[None, :]
    sines = jnp.sin(angles)
    return jnp.cos(angles), jnp.where(lane[None, :] % 2 == 0, -sines, sines)


def ring_order(count):
    if count > 8:
        return list(range(count))
    return list(range(0, count, 2)) + list(range(1, count, 2))[::-1]


def after(value, *earlier):
    return lax.optimization_barrier((value, *earlier))[0]


def program(count, rows, lengths, info, x, scale, wq, wkv, wdown, wup, index, mix):
    order = ring_order(count)
    reach = count // 2
    cw = [(order[i], order[(i + 1) % count]) for i in range(count)]
    ccw = [(b, a) for a, b in cw]
    send_cw = functools.partial(lax.ppermute, axis_name="tensor", perm=cw)
    send_ccw = functools.partial(lax.ppermute, axis_name="tensor", perm=ccw)

    opposite = [(order[i], order[(i + reach) % count]) for i in range(count)]

    cw_first, ccw_first, packed = scale_rows(lengths, info, x, scale, wkv, rows, reach)
    from_cw, from_ccw = [send_cw(cw_first), None], [send_ccw(ccw_first), None]
    low, side, cw_second, ccw_second, own = low_partials(
        lengths, info, x, packed, wdown, index, mix, wkv, rows, reach
    )
    from_cw[1], from_ccw[1] = send_cw(cw_second), send_ccw(ccw_second)
    done = low
    totals = [None, None]
    half = rows // 2
    pending = [[(0, packed, piece * half)] for piece in range(2)]

    for step in range(1, reach):
        final = step + 1 == reach
        for piece in range(2):
            got_cw, got_ccw, _ = lax.optimization_barrier((from_cw[piece], from_ccw[piece], done))
            aways = [reach - step - piece, count - reach + step + 1 - piece]
            ends = got_cw, got_ccw
            if final:
                moving, aways = [ends[piece]], [aways[piece]]
            else:
                moving = list(ends)
            if piece == 0:
                moved = add_terms(info, moving, aways, packed, wkv, rows)
            else:
                *moved, around = add_terms_low(info, moving, aways, packed, wkv, low, rows)
            if final and piece == 0:
                moved = [*moved, got_ccw]
            elif final:
                moved = [got_cw, *moved]
            if not (final and piece == 1):
                from_cw[piece] = send_cw(moved[0])
            else:
                from_cw[piece] = moved[0]
            if not (final and piece == 0):
                from_ccw[piece] = send_ccw(moved[1])
            else:
                from_ccw[piece] = moved[1]
            done = moved[piece]
            pending[piece] += [(count - step, moved[0], 0), (step, moved[1], 0)]
            if step == 1 and piece == 1:
                opposite_low = lax.ppermute(around, "tensor", opposite)
            if step == reach - 2 and piece == 1:
                late, _ = lax.optimization_barrier((opposite_low, done))
                delta, inv = query_delta(low, late, *ends, side, wup, wq.shape[0])
                done = delta
            else:
                ending = (delta, inv) if final else None
                totals[piece] = product(
                    info, totals[piece], pending[piece], wq, half, ending, piece if final else None
                )
                pending[piece] = []
                done = totals[piece]
    tables = rotation_tables()
    context = None
    for prompt in range(2):
        last = (from_cw[0], from_ccw[1])[prompt]
        kv = (own, from_cw[prompt], from_ccw[prompt])
        context = attention(
            info, lengths, totals[prompt], inv, last, reach, wq, kv, tables, prompt, context
        )
    return context


def shards(count, x, scale, wq, wkv, wdown, wup, index, mix, lengths):
    shard = lax.axis_index("tensor")
    order = ring_order(count)
    heads = wq.shape[1] // HEAD_WIDTH
    table = np.zeros((count, 2, count), np.int32)
    for place, device in enumerate(order):
        for i in range(count):
            other = order[(place + i) % count]
            table[device, 0, i] = other
            table[device, 1, i] = other * heads // (QUERY_HEADS // KV_HEADS)
    info = lax.dynamic_index_in_dim(jnp.asarray(table), shard, 0, keepdims=False)
    return program(count, x.shape[0], lengths, info, x, scale, wq, wkv, wdown, wup, index, mix)


def solution(mesh):
    placed = (
        P(("groups", "replica"), "tensor"),
        P(),
        P(None, "tensor"),
        P("tensor", None),
        P("tensor", None),
        P(None, "tensor"),
        P(("groups", "replica"), None),
        P(("groups", "replica"), None),
        P(("groups", "replica")),
    )
    return jax.shard_map(
        functools.partial(shards, mesh.shape["tensor"]),
        mesh=mesh,
        in_specs=placed,
        out_specs=P(("groups", "replica"), "tensor"),
        check_vma=False,
    )
```

```python
import functools
import math

import jax
import jax.numpy as jnp
import numpy as np
from jax import lax
from jax.experimental import pallas as pl
from jax.experimental.pallas import tpu as pltpu
from jax.sharding import PartitionSpec as P

QUERY_HEADS = 64
KV_HEADS = 8
HEAD_WIDTH = 128
ADAPTER_RANK = 16
SLOT = 256
LANES = 128
LOW_ROWS = 40

EPS = 1e-05
ROPE_BASE = 500000.0

SIDE_MIX = 0
SIDE_INDEX = 2

DEPTH = 3
CHUNK = 512
HEADS_AT_ONCE = 8
DELTA_TILE = 1024
ADD_WEIGHT = 8.0
QUERY_WEIGHT = 8.0
VMEM_LIMIT = 64 * 1024 * 1024 - 64 * 1024
F32 = jnp.float32
BF16 = jnp.bfloat16


def call(kernel, out_shape, microseconds=0.0, **kwargs):
    return pl.pallas_call(
        kernel,
        out_shape=out_shape,
        compiler_params=pltpu.CompilerParams(vmem_limit_bytes=VMEM_LIMIT),
        cost_estimate=pl.CostEstimate(
            flops=int(1.15e9 * microseconds), bytes_accessed=1000, transcendentals=0
        ),
        **kwargs,
    )


def whole(shape):
    return pl.BlockSpec(shape, lambda *_: (0,) * len(shape))


def shape_of(shape, dtype):
    return jax.ShapeDtypeStruct(shape, dtype)


def prefetch(count, grid, in_specs, out_specs, scratch_shapes=()):
    return pltpu.PrefetchScalarGridSpec(
        num_scalar_prefetch=count,
        grid=grid,
        in_specs=in_specs,
        out_specs=out_specs,
        scratch_shapes=scratch_shapes,
    )


def write_message(message, block, w_ref):
    half, width = block.shape
    message[:half, :width] = block
    product = jnp.dot(block, w_ref[...], preferred_element_type=F32)
    message[:half, width:] = product.astype(BF16)


def scale_kernel(info_ref, x_ref, scale_ref, cw_w_ref, ccw_w_ref, cw_ref, ccw_ref, packed):
    half = cw_ref.shape[0]
    packed[...] = (x_ref[...].astype(F32) * scale_ref[...]).astype(BF16)
    block = packed[:half, :]
    write_message(cw_ref, block, cw_w_ref)
    write_message(ccw_ref, block, ccw_w_ref)


def scale_rows(info, x, scale, weight, reach):
    tokens, width = x.shape
    pair = 2 * HEAD_WIDTH
    message = (tokens // 2, width + pair)
    column = [
        pl.BlockSpec((width, pair), lambda j, info, away=away: (0, info[1, away]))
        for away in (reach, reach + 1)
    ]
    return call(
        scale_kernel,
        (shape_of(message, BF16),) * 2 + (shape_of((tokens, width), BF16),),
        grid_spec=prefetch(
            1,
            (1,),
            [
                whole((tokens, width)),
                pl.BlockSpec((1, width), lambda j, info: (0, info[0, 0])),
                *column,
            ],
            (whole(message),) * 2 + (whole((tokens, width)),),
        ),
    )(info, x, scale.reshape(1, -1), weight, weight)


def low_places(tokens, full):
    if full >= 2 * tokens + SLOT:
        second = (slice(0, ADAPTER_RANK), slice(tokens, 2 * tokens))
        squares = (0, slice(2 * tokens, 2 * tokens + SLOT))
        extra = ADAPTER_RANK
    else:
        second = (slice(ADAPTER_RANK, 2 * ADAPTER_RANK), slice(0, tokens))
        squares = (2 * ADAPTER_RANK, slice(0, SLOT))
        extra = 3 * ADAPTER_RANK
    return extra, (slice(0, ADAPTER_RANK), slice(0, tokens)), second, squares


def read_low(region):
    tokens = 2 * SLOT
    _, first, second, (row, lanes) = low_places(tokens, region.shape[1])
    squares = jnp.concatenate(
        [region[row + i : row + i + 1, lanes] + region[row + 2 + i : row + 3 + i, lanes] for i in range(2)],
        axis=1,
    )
    return jnp.concatenate(
        [region[first], region[second], squares, jnp.zeros((LOW_ROWS - 33, tokens), F32)], axis=0
    )


def write_low(message, half, low):
    tokens = 2 * SLOT
    extra, first, second, (row, lanes) = low_places(tokens, message.shape[1])
    message[half : half + extra, :] = jnp.zeros((extra, message.shape[1]), BF16)
    squares = low[2 * ADAPTER_RANK : 2 * ADAPTER_RANK + 1, :]
    rounded = squares.astype(BF16)
    rest = (squares - rounded.astype(F32)).astype(BF16)
    for place, value in ((first, low[:ADAPTER_RANK]), (second, low[ADAPTER_RANK : 2 * ADAPTER_RANK])):
        span = slice(half + place[0].start, half + place[0].stop)
        message[span, place[1]] = value.astype(BF16)
    block = jnp.concatenate(
        [rounded[:, :SLOT], rounded[:, SLOT:], rest[:, :SLOT], rest[:, SLOT:]]
        + [jnp.zeros((ADAPTER_RANK - 4, SLOT), BF16)],
        axis=0,
    )
    message[half + row : half + row + ADAPTER_RANK, lanes] = block


def terms_kernel(info_ref, x_ref, ahead_w_ref, behind_w_ref, ahead_ref, behind_ref):
    for w_ref, out_ref in ((ahead_w_ref, ahead_ref), (behind_w_ref, behind_ref)):
        out_ref[0] = jnp.dot(x_ref[...], w_ref[...], preferred_element_type=F32).astype(BF16)


def late_terms(info, packed, weight, count):
    rows, width = packed.shape
    pair = 2 * HEAD_WIDTH
    number = count // 2 - 2
    out = shape_of((number, rows, pair), BF16)
    block = pl.BlockSpec((1, rows, pair), lambda i, info: (i, 0, 0))
    return call(
        terms_kernel,
        (out, out),
        grid_spec=prefetch(
            1,
            (number,),
            [
                whole((rows, width)),
                pl.BlockSpec((width, pair), lambda i, info: (0, info[1, 1 + i])),
                pl.BlockSpec((width, pair), lambda i, info: (0, info[1, count - 1 - i])),
            ],
            (block, block),
        ),
    )(info, packed, weight, weight)


def own_term(block_ref, w_ref):
    if block_ref is None:
        return w_ref[0].astype(F32)
    return jnp.dot(block_ref[...], w_ref[...], preferred_element_type=F32)


def term_specs(info, aways, packed, weight, terms, piece):
    rows, width = packed.shape
    half = rows // 2
    pair = 2 * HEAD_WIDTH
    if terms is None:
        specs = [pl.BlockSpec((half, width), lambda j, info: (piece, 0))]
        specs += [
            pl.BlockSpec((width, pair), lambda j, info, away=away: (0, info[1, away]))
            for away in aways
        ]
        return [packed] + [weight] * len(aways), specs
    count = info.shape[1]
    operands, specs = [], []
    for away in aways:
        ahead = away < count // 2
        operands.append(terms[0 if ahead else 1])
        place = away - 1 if ahead else count - 1 - away
        specs.append(pl.BlockSpec((1, half, pair), lambda j, info, place=place: (place, piece, 0)))
    return operands, specs


def add_kernel(ready, info_ref, *refs):
    refs = list(refs)
    messages = [refs.pop(0), refs.pop(0)]
    block = None if ready else refs.pop(0)
    for i, message in enumerate(messages):
        total = message[...].astype(F32) + own_term(block, refs[i])
        refs[2 + i][...] = total.astype(BF16)


def add_terms(info, messages, aways, packed, weight, terms, rows):
    half = rows // 2
    full = messages[0].shape[1]
    pair = 2 * HEAD_WIDTH
    lanes = pl.BlockSpec((half, pair), lambda j, info: (0, full // pair - 1))
    operands, specs = term_specs(info, aways, packed, weight, terms, 0)
    return call(
        functools.partial(add_kernel, terms is not None),
        (shape_of((half, full), BF16),) * 2,
        ADD_WEIGHT,
        grid_spec=prefetch(1, (1,), [lanes] * 2 + specs, (lanes,) * 2),
        input_output_aliases={1: 0, 2: 1},
    )(info, *messages, *operands)


def add_low_kernel(half, ready, info_ref, low_ref, *refs):
    refs = list(refs)
    pair = 2 * HEAD_WIDTH
    around = low_ref[...]
    messages = [refs.pop(0), refs.pop(0)]
    block = None if ready else refs.pop(0)
    for i, given in enumerate(messages):
        out = refs[2 + i]
        full = given.shape[1]
        out[:half, : full - pair] = given[:half, : full - pair]
        own = own_term(block, refs[i])
        out[:half, full - pair :] = (given[:half, full - pair :].astype(F32) + own).astype(BF16)
        if out.shape[0] > half:
            sums = read_low(given[half:, :].astype(F32))
            around = around + sums
            write_low(out, half, sums + low_ref[...])
    if len(refs) > 4:
        refs[4][...] = around


def add_terms_low(info, messages, aways, packed, weight, terms, low, rows, keep):
    half = rows // 2
    shape = messages[0].shape
    after = shape if keep else (half, shape[1])
    out = (shape_of(after, BF16),) * 2 + ((shape_of(low.shape, F32),) if keep else ())
    operands, specs = term_specs(info, aways, packed, weight, terms, 1)
    return call(
        functools.partial(add_low_kernel, half, terms is not None),
        out,
        ADD_WEIGHT,
        grid_spec=prefetch(
            1,
            (1,),
            [whole(low.shape)] + [whole(shape)] * 2 + specs,
            tuple(whole(each.shape) for each in out),
        ),
    )(info, low, *messages, *operands)


def last_kernel(half, ready, info_ref, with_sums, other, *refs):
    refs = list(refs)
    block = None if ready else refs.pop(0)
    term, first_ref, second_ref = refs
    width = second_ref.shape[1]
    mid = half // 2
    pair = 2 * HEAD_WIDTH
    own = own_term(block, term)
    sums = (with_sums[:half, width:].astype(F32) + own).astype(BF16)
    first_ref[:, :width] = with_sums[:mid, :width]
    first_ref[:, width : width + pair] = sums[:mid]
    first_ref[:, width + pair :] = sums[mid:]
    second_ref[...] = other[mid:half, :width]


def last_messages(info, with_sums, other, away, packed, weight, terms, rows, piece):
    half = rows // 2
    width = weight.shape[0]
    pair = 2 * HEAD_WIDTH
    out = (shape_of((half // 2, width + 2 * pair), BF16), shape_of((half // 2, width), BF16))
    operands, specs = term_specs(info, [away], packed, weight, terms, piece)
    return call(
        functools.partial(last_kernel, half, terms is not None),
        out,
        ADD_WEIGHT,
        grid_spec=prefetch(
            1,
            (1,),
            [whole(with_sums.shape), whole(other.shape)] + specs,
            tuple(whole(each.shape) for each in out),
        ),
    )(info, with_sums, other, *operands)


def chosen_group(index):
    rows = index.shape[0]
    lane = lax.broadcasted_iota(jnp.int32, (rows, LANES), 1)
    return index - (lane // ADAPTER_RANK).astype(F32)


def fold(value):
    shift = ADAPTER_RANK
    while shift < LANES:
        value = value + pltpu.roll(value, shift, 1)
        shift *= 2
    return value


def low_kernel(
    aways, info_ref, packed_ref, w_ref, index_ref, mix_ref, x_ref, kv_ref, out_ref, side_ref,
    cw_ref, ccw_ref, own_ref, acc_ref, group_ref, squares_ref, x_s, columns_s, messages_s, sems,
    out_sems,
):
    step = pl.program_id(0)
    tile = w_ref.shape[1]
    tokens = x_ref.shape[0]
    half = tokens // 2
    pair = 2 * HEAD_WIDTH
    reads = [pltpu.make_async_copy(x_ref, x_s, sems.at[0])]
    for i, away in enumerate(aways):
        first = pl.multiple_of(info_ref[1, away] * pair, pair)
        column = kv_ref.at[:, pl.ds(first, pair)]
        reads.append(pltpu.make_async_copy(column, columns_s.at[i], sems.at[1 + i]))
    writes = []
    for i, ref in enumerate((cw_ref, ccw_ref)):
        extra = ref.shape[0] - half
        for j, span in enumerate((pl.ds(0, half), pl.ds(half, extra))):
            block = messages_s.at[i, span]
            writes.append(pltpu.make_async_copy(block, ref.at[span], out_sems.at[i, j]))

    @pl.when(step == 0)
    def _():
        for copy in reads:
            copy.start()
        acc_ref[...] = jnp.zeros_like(acc_ref)
        side = jnp.concatenate(
            [mix_ref[...], index_ref[...].astype(F32), jnp.zeros((LANES - 4, tokens), F32)],
            axis=0,
        ).T
        side_ref[...] = side
        for k in range(2):
            group_ref[k] = chosen_group(side[:, SIDE_INDEX + k : SIDE_INDEX + k + 1])

    @pl.when(step == 1)
    def _():
        for copy in reads:
            copy.wait()
        x = x_s[...].astype(F32)
        squares = jnp.sum(x * x, axis=1, keepdims=True)
        squares_ref[...] = jnp.broadcast_to(squares, squares_ref.shape)
        for i in range(2):
            write_message(messages_s.at[i], packed_ref[half:, :], columns_s.at[i])
            writes[2 * i].start()
        own = jnp.dot(packed_ref[...], columns_s[2], preferred_element_type=F32)
        own_ref[...] = own.astype(BF16)

    chunk = min(CHUNK, tile)
    for first in range(0, tile, chunk):
        product = jnp.dot(
            packed_ref[...], w_ref[:, first : first + chunk], preferred_element_type=F32
        )
        for k in range(2):
            total = acc_ref[k]
            for s in range(chunk // LANES):
                group = (step * tile + first + s * LANES) // ADAPTER_RANK
                here = group_ref[k] == group.astype(F32)
                total += jnp.where(here, product[:, s * LANES : (s + 1) * LANES], 0.0)
            acc_ref[k] = total

    @pl.when(step == pl.num_programs(0) - 1)
    def _():
        lane = lax.broadcasted_iota(jnp.int32, (tokens, LANES), 1)
        sums = jnp.where(lane < ADAPTER_RANK, fold(acc_ref[0]), fold(acc_ref[1]))
        sums = jnp.where(lane < 2 * ADAPTER_RANK, sums, 0.0)
        sums = jnp.where(lane == 2 * ADAPTER_RANK, squares_ref[...], sums)
        low = sums.T[:LOW_ROWS]
        out_ref[...] = low
        for i in range(2):
            write_low(messages_s.at[i], half, low)
            writes[2 * i + 1].start()
        for copy in writes:
            copy.wait()


def low_partials(info, x, packed, weight, index, mix, kv_weight, reach):
    width, columns = weight.shape
    tile = min(1024, columns)
    tokens = x.shape[0]
    pair = 2 * HEAD_WIDTH
    message = (tokens // 2 + low_places(tokens, width + pair)[0], width + pair)
    anywhere = pl.BlockSpec(memory_space=pl.ANY)
    return call(
        functools.partial(low_kernel, (reach - 1, reach, 0)),
        (shape_of((LOW_ROWS, tokens), F32), shape_of((tokens, LANES), F32))
        + (shape_of(message, BF16),) * 2
        + (shape_of((tokens, pair), BF16),),
        grid_spec=prefetch(
            1,
            (columns // tile,),
            [
                whole((tokens, width)),
                pl.BlockSpec((width, tile), lambda j, info: (0, j)),
                whole((2, tokens)),
                whole((2, tokens)),
                anywhere,
                anywhere,
            ],
            (whole((LOW_ROWS, tokens)), whole((tokens, LANES)), anywhere, anywhere)
            + (whole((tokens, pair)),),
            [
                pltpu.VMEM((2, tokens, LANES), F32),
                pltpu.VMEM((2, tokens, LANES), F32),
                pltpu.VMEM((tokens, LANES), F32),
                pltpu.VMEM((tokens, width), BF16),
                pltpu.VMEM((3, width, pair), BF16),
                pltpu.VMEM((2, *message), BF16),
                pltpu.SemaphoreType.DMA((4,)),
                pltpu.SemaphoreType.DMA((2, 2)),
            ],
        ),
    )(info, packed, weight, index.T, mix.T, x, kv_weight)


def delta_kernel(
    model_width, slots, info_ref, low_ref, opposite_ref, cw_ref, ccw_ref, total_a_ref, total_b_ref,
    weight_ref, side_ref, w_ref, out_a_ref, out_b_ref, inv_ref, co_ref, group_ref, ends, x_buf,
    w_buf, sems,
):
    step = pl.program_id(0)
    tile = w_ref.shape[0]
    half, width = x_buf.shape[1:]
    outs = (out_a_ref, out_b_ref)
    messages = (cw_ref, ccw_ref)
    end_copies = [
        pltpu.make_async_copy(ref.at[pl.ds(half, ends.shape[1])], ends.at[i], sems.at[i])
        for i, ref in enumerate(messages)
    ]
    total_copies = [
        pltpu.make_async_copy(ref, outs[i], sems.at[2 + i])
        for i, ref in enumerate((total_a_ref, total_b_ref))
    ]
    row_copies = [
        pltpu.make_async_copy(
            ref.at[pl.ds(0, half), pl.ds(0, width)], x_buf.at[i], sems.at[4 + i]
        )
        for i, ref in enumerate(messages)
    ]
    weight_copies = []
    for i in range(2):
        first = pl.multiple_of(info_ref[0, slots[i]] * width, width)
        block = weight_ref.at[pl.ds(first, width)]
        weight_copies.append(pltpu.make_async_copy(block, w_buf.at[i], sems.at[6 + i]))

    @pl.when(step == 0)
    def _():
        for copy in end_copies + total_copies + row_copies + weight_copies:
            copy.start()
        for k in range(2):
            group_ref[k] = chosen_group(side_ref[:, SIDE_INDEX + k : SIDE_INDEX + k + 1])
        for copy in end_copies:
            copy.wait()
        tokens = low_ref.shape[1]
        sums = low_ref[...] + opposite_ref[...]
        for i in range(2):
            sums = sums + read_low(ends[i].astype(F32))
        padding = jnp.zeros((LANES - LOW_ROWS, tokens), F32)
        low = jnp.concatenate([sums, padding], axis=0).T
        lane = lax.broadcasted_iota(jnp.int32, (tokens, LANES), 1)
        squares = low[:, 2 * ADAPTER_RANK : 2 * ADAPTER_RANK + 1]
        inverse = lax.rsqrt(squares * (1.0 / model_width) + EPS)
        inv_ref[...] = jnp.broadcast_to(inverse, (tokens, LANES))
        for k in range(2):
            value = fold(jnp.where(lane // ADAPTER_RANK == k, low, 0.0))
            co_ref[k] = value * inverse * side_ref[:, SIDE_MIX + k : SIDE_MIX + k + 1]
        for i in range(2):
            total_copies[i].wait()
            outs[i][...] = outs[i][...] * inverse[i * half : (i + 1) * half]

    pieces = []
    for s in range(tile // LANES):
        group = ((step * tile + s * LANES) // ADAPTER_RANK).astype(F32)
        piece = jnp.where(group_ref[0] == group, co_ref[0], 0.0)
        piece = jnp.where(group_ref[1] == group, co_ref[1], piece)
        pieces.append(piece.astype(BF16))
    coefficients = jnp.concatenate(pieces, axis=1)
    product = jnp.dot(coefficients, w_ref[...], preferred_element_type=F32)
    for i in range(2):
        outs[i][...] += product[i * half : (i + 1) * half]

    @pl.when(step == pl.num_programs(0) - 1)
    def _():
        for i in range(2):
            row_copies[i].wait()
            weight_copies[i].wait()
            product = jnp.dot(x_buf[i], w_buf[i], preferred_element_type=F32)
            out_b_ref[...] += product * inv_ref[half:, 0:1]


def query_delta(info, low, opposite, messages, slots, totals, weight, side, up):
    depth, columns = up.shape
    tile = min(DELTA_TILE, depth)
    tokens = side.shape[0]
    half = tokens // 2
    full = messages[0].shape[1]
    width = weight.shape[0] // info.shape[1]
    anywhere = pl.BlockSpec(memory_space=pl.ANY)
    extra = low_places(tokens, full)[0]
    return call(
        functools.partial(delta_kernel, weight.shape[0], slots),
        (shape_of((half, columns), F32),) * 2 + (shape_of((tokens, LANES), F32),),
        QUERY_WEIGHT,
        grid_spec=prefetch(
            1,
            (depth // tile,),
            [whole(low.shape), whole(low.shape)]
            + [anywhere] * 5
            + [whole(side.shape), pl.BlockSpec((tile, columns), lambda j, _: (j, 0))],
            (whole((half, columns)), whole((half, columns)), whole((tokens, LANES))),
            [
                pltpu.VMEM((2, tokens, LANES), F32),
                pltpu.VMEM((2, tokens, LANES), F32),
                pltpu.VMEM((2, extra, full), BF16),
                pltpu.VMEM((2, half, width), BF16),
                pltpu.VMEM((2, width, columns), BF16),
                pltpu.SemaphoreType.DMA((8,)),
            ],
        ),
    )(info, low, opposite, *messages, *totals, weight, side, up)


def product_kernel(slots, starts, has_total, has_inv, info_ref, *refs):
    refs = list(refs)
    count = len(slots)
    blocks = [refs.pop(0) for _ in range(count)]
    weight = refs.pop(0)
    total_ref = refs.pop(0) if has_total else None
    inv_ref = refs.pop(0) if has_inv else None
    out_ref, x_buf, w_buf, sems, total_sem = refs
    depth, half, width = x_buf.shape
    columns = w_buf.shape[2]
    chunk = min(CHUNK, columns)

    def copies(i):
        buf = i % depth
        first = pl.multiple_of(info_ref[0, slots[i]] * width, width)
        block = blocks[i].at[pl.ds(starts[i], half), pl.ds(0, width)]
        return [
            pltpu.make_async_copy(weight.at[pl.ds(first, width)], w_buf.at[buf], sems.at[buf, 0]),
            pltpu.make_async_copy(block, x_buf.at[buf], sems.at[buf, 1]),
        ]

    for i in range(min(depth - 1, count)):
        for copy in copies(i):
            copy.start()
    if has_total:
        total_copy = pltpu.make_async_copy(total_ref, out_ref, total_sem)
        total_copy.start()
    for i in range(count):
        buf = i % depth
        if i + depth - 1 < count:
            for copy in copies(i + depth - 1):
                copy.start()
        for copy in copies(i):
            copy.wait()
        if i == 0 and has_total:
            total_copy.wait()
        for first in range(0, columns, chunk):
            span = slice(first, first + chunk)
            value = jnp.dot(x_buf[buf], w_buf[buf, :, span], preferred_element_type=F32)
            if has_inv:
                value = value * inv_ref[:, 0:1]
            if i > 0 or has_total:
                value = out_ref[:, span] + value
            out_ref[:, span] = value


def product(info, total, sources, weight, half, inv=None, place=0):
    columns = weight.shape[1]
    width = weight.shape[0] // info.shape[1]
    operands = [block for _, block, _ in sources] + [weight] + ([] if total is None else [total])
    in_specs = [pl.BlockSpec(memory_space=pl.ANY)] * len(operands)
    if inv is not None:
        operands.append(inv)
        in_specs.append(pl.BlockSpec((half, LANES), lambda j, info: (place, 0)))
    slots = [slot for slot, _, _ in sources]
    starts = [start for _, _, start in sources]
    return call(
        functools.partial(product_kernel, slots, starts, total is not None, inv is not None),
        shape_of((half, columns), F32),
        QUERY_WEIGHT,
        grid_spec=prefetch(
            1,
            (1,),
            in_specs,
            whole((half, columns)),
            [
                pltpu.VMEM((DEPTH, half, width), BF16),
                pltpu.VMEM((DEPTH, width, columns), BF16),
                pltpu.SemaphoreType.DMA((DEPTH, 2)),
                pltpu.SemaphoreType.DMA,
            ],
        ),
    )(info, *operands)


def rotate(values, cosines, sines):
    lane = lax.broadcasted_iota(jnp.int32, values.shape, 1)
    after = pltpu.roll(values, LANES - 1, 1)
    before = pltpu.roll(values, 1, 1)
    other = jnp.where(lane % 2 == 0, after, before)
    return values * cosines + other * sines


def attention_kernel(
    info_ref, lengths_ref, total_a_ref, total_b_ref, inv_ref, w_ref, cos_ref, sin_ref, own_ref,
    *refs,
):
    parts, sums = refs[:4], refs[4:10]
    out_ref, last_s, key_s, value_s, bias_s = refs[10:]
    mid = parts[0].shape[0]

    @pl.when(pl.program_id(0) == 0)
    def _():
        row = lax.broadcasted_iota(jnp.int32, (SLOT, SLOT), 0)
        col = lax.broadcasted_iota(jnp.int32, (SLOT, SLOT), 1)
        for i, part in enumerate(parts):
            last_s[i * mid : (i + 1) * mid, :] = part[...]
        for prompt in range(2):
            span = slice(prompt * SLOT, (prompt + 1) * SLOT)
            first, second, other = sums[3 * prompt : 3 * prompt + 3]
            pair = jnp.concatenate([first[...], second[...]], axis=0).astype(F32)
            pair = pair + other[...].astype(F32) + own_ref[span, :].astype(F32)
            pair = pair * inv_ref[span, 0:1]
            key = rotate(pair[:, :HEAD_WIDTH], cos_ref[...], sin_ref[...])
            key_s[prompt] = key.astype(BF16)
            value_s[prompt] = pair[:, HEAD_WIDTH:].astype(BF16)
            seen = (col <= row) & (col < lengths_ref[prompt])
            bias_s[prompt] = jnp.where(seen, 0.0, -1e30)

    product = jnp.dot(last_s[...], w_ref[...], preferred_element_type=F32)
    row_narrow = lax.broadcasted_iota(jnp.int32, (SLOT, HEAD_WIDTH), 0)
    factor = math.log2(math.e) / math.sqrt(HEAD_WIDTH)
    for prompt, total_ref in enumerate((total_a_ref, total_b_ref)):
        rows = slice(prompt * SLOT, (prompt + 1) * SLOT)
        queries = total_ref[...] + product[rows] * inv_ref[rows, 0:1]
        for head in range(w_ref.shape[1] // HEAD_WIDTH):
            span = slice(head * HEAD_WIDTH, (head + 1) * HEAD_WIDTH)
            query = rotate(queries[:, span], cos_ref[...], sin_ref[...]).astype(BF16)
            scores = lax.dot_general(
                query, key_s[prompt], (((1,), (1,)), ((), ())), preferred_element_type=F32
            )
            scores = scores * factor + bias_s[prompt]
            top = jnp.max(scores, axis=1, keepdims=True)
            weights = jnp.exp2(scores - top)
            totals = jnp.sum(weights, axis=1, keepdims=True)
            mixed = jnp.dot(weights.astype(BF16), value_s[prompt], preferred_element_type=F32)
            mixed = jnp.where(row_narrow < lengths_ref[prompt], mixed * (1.0 / totals), 0.0)
            out_ref[rows, span] = mixed.astype(BF16)


def attention(info, lengths, totals, inv, last_slot, weight, own, parts, tables):
    width = weight.shape[0] // info.shape[1]
    columns = weight.shape[1]
    tile = min(HEADS_AT_ONCE * HEAD_WIDTH, columns)
    pair = 2 * HEAD_WIDTH
    mid = SLOT // 2
    tokens = 2 * SLOT
    rows_of = [part for first, second, _ in parts for part in (first, second)]
    sums_of = [part for first, _, other in parts for part in (first, first, other)]
    lane = width // pair
    sums_specs = [
        pl.BlockSpec((mid, pair), lambda j, *_: (0, lane)),
        pl.BlockSpec((mid, pair), lambda j, *_: (0, lane + 1)),
        pl.BlockSpec((SLOT, pair), lambda j, *_: (0, lane)),
    ]
    return call(
        attention_kernel,
        shape_of((tokens, columns), BF16),
        grid_spec=prefetch(
            2,
            (columns // tile,),
            [
                pl.BlockSpec((SLOT, tile), lambda j, *_: (0, j)),
                pl.BlockSpec((SLOT, tile), lambda j, *_: (0, j)),
                whole((tokens, LANES)),
                pl.BlockSpec((width, tile), lambda j, info, _: (info[0, last_slot], j)),
                whole((SLOT, HEAD_WIDTH)),
                whole((SLOT, HEAD_WIDTH)),
                whole((tokens, pair)),
            ]
            + [pl.BlockSpec((mid, width), lambda j, *_: (0, 0))] * 4
            + sums_specs * 2,
            pl.BlockSpec((tokens, tile), lambda j, *_: (0, j)),
            [
                pltpu.VMEM((tokens, width), BF16),
                pltpu.VMEM((2, SLOT, HEAD_WIDTH), BF16),
                pltpu.VMEM((2, SLOT, HEAD_WIDTH), BF16),
                pltpu.VMEM((2, SLOT, SLOT), F32),
            ],
        ),
    )(info, lengths, *totals, inv, weight, *tables, own, *rows_of, *sums_of)


def rotation_tables():
    lane = jnp.arange(HEAD_WIDTH)
    inverse = jnp.power(F32(ROPE_BASE), -2.0 * (lane // 2).astype(F32) / HEAD_WIDTH)
    angles = jnp.arange(SLOT).astype(F32)[:, None] * inverse[None, :]
    sines = jnp.sin(angles)
    return jnp.cos(angles), jnp.where(lane[None, :] % 2 == 0, -sines, sines)


def ring_order(count):
    if count > 8:
        return list(range(count))
    return list(range(0, count, 2)) + list(range(1, count, 2))[::-1]


def after(value, *earlier):
    return lax.optimization_barrier((value, *earlier))[0]


def program(count, rows, lengths, info, x, scale, wq, wkv, wdown, wup, index, mix):
    order = ring_order(count)
    reach = count // 2
    cw = [(order[i], order[(i + 1) % count]) for i in range(count)]
    ccw = [(b, a) for a, b in cw]
    send_cw = functools.partial(lax.ppermute, axis_name="tensor", perm=cw)
    send_ccw = functools.partial(lax.ppermute, axis_name="tensor", perm=ccw)

    opposite = [(order[i], order[(i + reach) % count]) for i in range(count)]

    cw_first, ccw_first, packed = scale_rows(info, x, scale, wkv, reach)
    from_cw, from_ccw = [send_cw(cw_first), None], [send_ccw(ccw_first), None]
    low, side, cw_second, ccw_second, own = low_partials(
        info, x, packed, wdown, index, mix, wkv, reach
    )
    from_cw[1], from_ccw[1] = send_cw(cw_second), send_ccw(ccw_second)
    done = low
    totals = [None, None]
    inv = None
    last = []
    terms = None
    half = rows // 2

    for step in range(1, reach):
        final = step + 1 == reach
        for piece in range(2):
            got_cw, got_ccw, _ = lax.optimization_barrier((from_cw[piece], from_ccw[piece], done))
            aways = [reach - step - piece, count - reach + step + 1 - piece]
            ends = got_cw, got_ccw
            moved = list(ends)
            if final:
                sums_from, other = ends if piece == 0 else ends[::-1]
                first, second = last_messages(
                    info, sums_from, other, aways[piece], packed, wkv, terms, rows, piece
                )
                if piece == 0:
                    last.append((send_cw(first), send_ccw(second), got_ccw))
                else:
                    last.append((send_ccw(first), send_cw(second), got_cw))
                done = first
            else:
                if piece == 0:
                    moved = add_terms(info, moved, aways, packed, wkv, terms, rows)
                else:
                    moved = add_terms_low(
                        info, moved, aways, packed, wkv, terms, low, rows, step < reach - 2
                    )
                from_cw[piece], from_ccw[piece] = send_cw(moved[0]), send_ccw(moved[1])
                done = moved[piece]
            sources = [(count - step, moved[0], 0), (step, moved[1], 0)]
            if step == 1:
                sources = [(0, packed, piece * half)] + sources
            if step == 1 and piece == 1:
                opposite_low = lax.ppermute(moved[2], "tensor", opposite)
            if step == reach - 2 and piece == 1:
                late, _ = lax.optimization_barrier((opposite_low, done))
                *totals, inv = query_delta(
                    info, low, late, ends, (count - step, step), totals, wq, side, wup
                )
                done = inv
            else:
                totals[piece] = product(info, totals[piece], sources, wq, half, inv, piece)
                done = totals[piece]
            if step == 1 and piece == 0:
                late = late_terms(info, after(packed, done), wkv, count)
                done = late[0]
            if step == 1 and piece == 1:
                terms = late
    return attention(info, lengths, totals, inv, reach, wq, own, last, rotation_tables())


def shards(count, x, scale, wq, wkv, wdown, wup, index, mix, lengths):
    shard = lax.axis_index("tensor")
    order = ring_order(count)
    heads = wq.shape[1] // HEAD_WIDTH
    table = np.zeros((count, 2, count), np.int32)
    for place, device in enumerate(order):
        for i in range(count):
            other = order[(place + i) % count]
            table[device, 0, i] = other
            table[device, 1, i] = other * heads // (QUERY_HEADS // KV_HEADS)
    info = lax.dynamic_index_in_dim(jnp.asarray(table), shard, 0, keepdims=False)
    return program(count, x.shape[0], lengths, info, x, scale, wq, wkv, wdown, wup, index, mix)


def solution(mesh):
    placed = (
        P(("groups", "replica"), "tensor"),
        P(),
        P(None, "tensor"),
        P("tensor", None),
        P("tensor", None),
        P(None, "tensor"),
        P(("groups", "replica"), None),
        P(("groups", "replica"), None),
        P(("groups", "replica")),
    )
    return jax.shard_map(
        functools.partial(shards, mesh.shape["tensor"]),
        mesh=mesh,
        in_specs=placed,
        out_specs=P(("groups", "replica"), "tensor"),
        check_vma=False,
    )
```

```python
import functools
import math

import jax
import jax.numpy as jnp
import numpy as np
from jax import lax
from jax.experimental import pallas as pl
from jax.experimental.pallas import tpu as pltpu
from jax.sharding import PartitionSpec as P

QUERY_HEADS = 64
KV_HEADS = 8
HEAD_WIDTH = 128
ADAPTER_RANK = 16
SLOT = 256
LANES = 128
LOW_ROWS = 40

EPS = 1e-05
ROPE_BASE = 500000.0

SIDE_MIX = 0
SIDE_INDEX = 2

DEPTH = 3
CHUNK = 512
HEADS_AT_ONCE = 8
DELTA_TILE = 1024
ADD_WEIGHT = 8.0
QUERY_WEIGHT = 8.0
VMEM_LIMIT = 64 * 1024 * 1024 - 64 * 1024
F32 = jnp.float32
BF16 = jnp.bfloat16


def call(kernel, out_shape, microseconds=0.0, **kwargs):
    return pl.pallas_call(
        kernel,
        out_shape=out_shape,
        compiler_params=pltpu.CompilerParams(vmem_limit_bytes=VMEM_LIMIT),
        cost_estimate=pl.CostEstimate(
            flops=int(1.15e9 * microseconds), bytes_accessed=1000, transcendentals=0
        ),
        **kwargs,
    )


def whole(shape):
    return pl.BlockSpec(shape, lambda *_: (0,) * len(shape))


def shape_of(shape, dtype):
    return jax.ShapeDtypeStruct(shape, dtype)


def prefetch(count, grid, in_specs, out_specs, scratch_shapes=()):
    return pltpu.PrefetchScalarGridSpec(
        num_scalar_prefetch=count,
        grid=grid,
        in_specs=in_specs,
        out_specs=out_specs,
        scratch_shapes=scratch_shapes,
    )


def write_message(message, block, w_ref):
    half, width = block.shape
    message[:half, :width] = block
    product = jnp.dot(block, w_ref[...], preferred_element_type=F32)
    message[:half, width:] = product.astype(BF16)


def scale_kernel(info_ref, x_ref, scale_ref, cw_w_ref, ccw_w_ref, cw_ref, ccw_ref, packed):
    half = cw_ref.shape[0]
    packed[...] = (x_ref[...].astype(F32) * scale_ref[...]).astype(BF16)
    block = packed[:half, :]
    write_message(cw_ref, block, cw_w_ref)
    write_message(ccw_ref, block, ccw_w_ref)


def scale_rows(info, x, scale, weight, reach):
    tokens, width = x.shape
    pair = 2 * HEAD_WIDTH
    message = (tokens // 2, width + pair)
    column = [
        pl.BlockSpec((width, pair), lambda j, info, away=away: (0, info[1, away]))
        for away in (reach, reach + 1)
    ]
    return call(
        scale_kernel,
        (shape_of(message, BF16),) * 2 + (shape_of((tokens, width), BF16),),
        grid_spec=prefetch(
            1,
            (1,),
            [
                whole((tokens, width)),
                pl.BlockSpec((1, width), lambda j, info: (0, info[0, 0])),
                *column,
            ],
            (whole(message),) * 2 + (whole((tokens, width)),),
        ),
    )(info, x, scale.reshape(1, -1), weight, weight)


def low_places(tokens, full):
    if full >= 2 * tokens + SLOT:
        second = (slice(0, ADAPTER_RANK), slice(tokens, 2 * tokens))
        squares = (0, slice(2 * tokens, 2 * tokens + SLOT))
        extra = ADAPTER_RANK
    else:
        second = (slice(ADAPTER_RANK, 2 * ADAPTER_RANK), slice(0, tokens))
        squares = (2 * ADAPTER_RANK, slice(0, SLOT))
        extra = 3 * ADAPTER_RANK
    return extra, (slice(0, ADAPTER_RANK), slice(0, tokens)), second, squares


def read_low(region):
    tokens = 2 * SLOT
    _, first, second, (row, lanes) = low_places(tokens, region.shape[1])
    squares = jnp.concatenate(
        [region[row + i : row + i + 1, lanes] + region[row + 2 + i : row + 3 + i, lanes] for i in range(2)],
        axis=1,
    )
    return jnp.concatenate(
        [region[first], region[second], squares, jnp.zeros((LOW_ROWS - 33, tokens), F32)], axis=0
    )


def write_low(message, half, low):
    tokens = 2 * SLOT
    extra, first, second, (row, lanes) = low_places(tokens, message.shape[1])
    message[half : half + extra, :] = jnp.zeros((extra, message.shape[1]), BF16)
    squares = low[2 * ADAPTER_RANK : 2 * ADAPTER_RANK + 1, :]
    rounded = squares.astype(BF16)
    rest = (squares - rounded.astype(F32)).astype(BF16)
    for place, value in ((first, low[:ADAPTER_RANK]), (second, low[ADAPTER_RANK : 2 * ADAPTER_RANK])):
        span = slice(half + place[0].start, half + place[0].stop)
        message[span, place[1]] = value.astype(BF16)
    block = jnp.concatenate(
        [rounded[:, :SLOT], rounded[:, SLOT:], rest[:, :SLOT], rest[:, SLOT:]]
        + [jnp.zeros((ADAPTER_RANK - 4, SLOT), BF16)],
        axis=0,
    )
    message[half + row : half + row + ADAPTER_RANK, lanes] = block


def terms_kernel(
    info_ref, x_ref, ahead_w_ref, behind_w_ref, own_w_ref, ahead_ref, behind_ref, own_ref
):
    @pl.when(pl.program_id(0) == 0)
    def _():
        own = jnp.dot(x_ref[...], own_w_ref[...], preferred_element_type=F32)
        own_ref[...] = own.astype(BF16)

    for w_ref, out_ref in ((ahead_w_ref, ahead_ref), (behind_w_ref, behind_ref)):
        out_ref[0] = jnp.dot(x_ref[...], w_ref[...], preferred_element_type=F32).astype(BF16)


def late_terms(info, packed, weight, count):
    rows, width = packed.shape
    pair = 2 * HEAD_WIDTH
    number = count // 2 - 2
    out = shape_of((number, rows, pair), BF16)
    block = pl.BlockSpec((1, rows, pair), lambda i, info: (i, 0, 0))
    return call(
        terms_kernel,
        (out, out, shape_of((rows, pair), BF16)),
        grid_spec=prefetch(
            1,
            (number,),
            [
                whole((rows, width)),
                pl.BlockSpec((width, pair), lambda i, info: (0, info[1, 1 + i])),
                pl.BlockSpec((width, pair), lambda i, info: (0, info[1, count - 1 - i])),
                pl.BlockSpec((width, pair), lambda i, info: (0, info[1, 0])),
            ],
            (block, block, whole((rows, pair))),
        ),
    )(info, packed, weight, weight, weight)


def own_term(block_ref, w_ref):
    if block_ref is None:
        return w_ref[0].astype(F32)
    return jnp.dot(block_ref[...], w_ref[...], preferred_element_type=F32)


def term_specs(info, aways, packed, weight, terms, piece):
    rows, width = packed.shape
    half = rows // 2
    pair = 2 * HEAD_WIDTH
    if terms is None:
        specs = [pl.BlockSpec((half, width), lambda j, info: (piece, 0))]
        specs += [
            pl.BlockSpec((width, pair), lambda j, info, away=away: (0, info[1, away]))
            for away in aways
        ]
        return [packed] + [weight] * len(aways), specs
    count = info.shape[1]
    operands, specs = [], []
    for away in aways:
        ahead = away < count // 2
        operands.append(terms[0 if ahead else 1])
        place = away - 1 if ahead else count - 1 - away
        specs.append(pl.BlockSpec((1, half, pair), lambda j, info, place=place: (place, piece, 0)))
    return operands, specs


def add_kernel(ready, info_ref, *refs):
    refs = list(refs)
    messages = [refs.pop(0), refs.pop(0)]
    block = None if ready else refs.pop(0)
    for i, message in enumerate(messages):
        total = message[...].astype(F32) + own_term(block, refs[i])
        refs[2 + i][...] = total.astype(BF16)


def add_terms(info, messages, aways, packed, weight, terms, rows):
    half = rows // 2
    full = messages[0].shape[1]
    pair = 2 * HEAD_WIDTH
    lanes = pl.BlockSpec((half, pair), lambda j, info: (0, full // pair - 1))
    operands, specs = term_specs(info, aways, packed, weight, terms, 0)
    return call(
        functools.partial(add_kernel, terms is not None),
        (shape_of((half, full), BF16),) * 2,
        ADD_WEIGHT,
        grid_spec=prefetch(1, (1,), [lanes] * 2 + specs, (lanes,) * 2),
        input_output_aliases={1: 0, 2: 1},
    )(info, *messages, *operands)


def add_low_kernel(half, ready, info_ref, low_ref, *refs):
    refs = list(refs)
    pair = 2 * HEAD_WIDTH
    around = low_ref[...]
    messages = [refs.pop(0), refs.pop(0)]
    block = None if ready else refs.pop(0)
    for i, given in enumerate(messages):
        out = refs[2 + i]
        full = given.shape[1]
        out[:half, : full - pair] = given[:half, : full - pair]
        own = own_term(block, refs[i])
        out[:half, full - pair :] = (given[:half, full - pair :].astype(F32) + own).astype(BF16)
        if out.shape[0] > half:
            sums = read_low(given[half:, :].astype(F32))
            around = around + sums
            write_low(out, half, sums + low_ref[...])
    if len(refs) > 4:
        refs[4][...] = around


def add_terms_low(info, messages, aways, packed, weight, terms, low, rows, keep):
    half = rows // 2
    shape = messages[0].shape
    after = shape if keep else (half, shape[1])
    out = (shape_of(after, BF16),) * 2 + ((shape_of(low.shape, F32),) if keep else ())
    operands, specs = term_specs(info, aways, packed, weight, terms, 1)
    return call(
        functools.partial(add_low_kernel, half, terms is not None),
        out,
        ADD_WEIGHT,
        grid_spec=prefetch(
            1,
            (1,),
            [whole(low.shape)] + [whole(shape)] * 2 + specs,
            tuple(whole(each.shape) for each in out),
        ),
    )(info, low, *messages, *operands)


def last_kernel(half, ready, info_ref, with_sums, other, *refs):
    refs = list(refs)
    block = None if ready else refs.pop(0)
    term, first_ref, second_ref = refs
    width = second_ref.shape[1]
    mid = half // 2
    pair = 2 * HEAD_WIDTH
    own = own_term(block, term)
    sums = (with_sums[:half, width:].astype(F32) + own).astype(BF16)
    first_ref[:, :width] = with_sums[:mid, :width]
    first_ref[:, width : width + pair] = sums[:mid]
    first_ref[:, width + pair :] = sums[mid:]
    second_ref[...] = other[mid:half, :width]


def last_messages(info, with_sums, other, away, packed, weight, terms, rows, piece):
    half = rows // 2
    width = weight.shape[0]
    pair = 2 * HEAD_WIDTH
    out = (shape_of((half // 2, width + 2 * pair), BF16), shape_of((half // 2, width), BF16))
    operands, specs = term_specs(info, [away], packed, weight, terms, piece)
    return call(
        functools.partial(last_kernel, half, terms is not None),
        out,
        ADD_WEIGHT,
        grid_spec=prefetch(
            1,
            (1,),
            [whole(with_sums.shape), whole(other.shape)] + specs,
            tuple(whole(each.shape) for each in out),
        ),
    )(info, with_sums, other, *operands)


def chosen_group(index):
    rows = index.shape[0]
    lane = lax.broadcasted_iota(jnp.int32, (rows, LANES), 1)
    return index - (lane // ADAPTER_RANK).astype(F32)


def fold(value):
    shift = ADAPTER_RANK
    while shift < LANES:
        value = value + pltpu.roll(value, shift, 1)
        shift *= 2
    return value


def low_kernel(
    aways, info_ref, packed_ref, w_ref, index_ref, mix_ref, x_ref, kv_ref, out_ref, side_ref,
    cw_ref, ccw_ref, acc_ref, group_ref, squares_ref, x_s, columns_s, messages_s, sems,
    out_sems,
):
    step = pl.program_id(0)
    tile = w_ref.shape[1]
    tokens = x_ref.shape[0]
    half = tokens // 2
    pair = 2 * HEAD_WIDTH
    reads = [pltpu.make_async_copy(x_ref, x_s, sems.at[0])]
    for i, away in enumerate(aways):
        first = pl.multiple_of(info_ref[1, away] * pair, pair)
        column = kv_ref.at[:, pl.ds(first, pair)]
        reads.append(pltpu.make_async_copy(column, columns_s.at[i], sems.at[1 + i]))
    writes = []
    for i, ref in enumerate((cw_ref, ccw_ref)):
        extra = ref.shape[0] - half
        for j, span in enumerate((pl.ds(0, half), pl.ds(half, extra))):
            block = messages_s.at[i, span]
            writes.append(pltpu.make_async_copy(block, ref.at[span], out_sems.at[i, j]))

    @pl.when(step == 0)
    def _():
        for copy in reads:
            copy.start()
        acc_ref[...] = jnp.zeros_like(acc_ref)
        side = jnp.concatenate(
            [mix_ref[...], index_ref[...].astype(F32), jnp.zeros((LANES - 4, tokens), F32)],
            axis=0,
        ).T
        side_ref[...] = side
        for k in range(2):
            group_ref[k] = chosen_group(side[:, SIDE_INDEX + k : SIDE_INDEX + k + 1])

    @pl.when(step == 1)
    def _():
        for copy in reads:
            copy.wait()
        x = x_s[...].astype(F32)
        squares = jnp.sum(x * x, axis=1, keepdims=True)
        squares_ref[...] = jnp.broadcast_to(squares, squares_ref.shape)
        for i in range(2):
            write_message(messages_s.at[i], packed_ref[half:, :], columns_s.at[i])
            writes[2 * i].start()
    chunk = min(CHUNK, tile)
    for first in range(0, tile, chunk):
        product = jnp.dot(
            packed_ref[...], w_ref[:, first : first + chunk], preferred_element_type=F32
        )
        for k in range(2):
            total = acc_ref[k]
            for s in range(chunk // LANES):
                group = (step * tile + first + s * LANES) // ADAPTER_RANK
                here = group_ref[k] == group.astype(F32)
                total += jnp.where(here, product[:, s * LANES : (s + 1) * LANES], 0.0)
            acc_ref[k] = total

    @pl.when(step == pl.num_programs(0) - 1)
    def _():
        lane = lax.broadcasted_iota(jnp.int32, (tokens, LANES), 1)
        sums = jnp.where(lane < ADAPTER_RANK, fold(acc_ref[0]), fold(acc_ref[1]))
        sums = jnp.where(lane < 2 * ADAPTER_RANK, sums, 0.0)
        sums = jnp.where(lane == 2 * ADAPTER_RANK, squares_ref[...], sums)
        low = sums.T[:LOW_ROWS]
        out_ref[...] = low
        for i in range(2):
            write_low(messages_s.at[i], half, low)
            writes[2 * i + 1].start()
        for copy in writes:
            copy.wait()


def low_partials(info, x, packed, weight, index, mix, kv_weight, reach):
    width, columns = weight.shape
    tile = min(1024, columns)
    tokens = x.shape[0]
    pair = 2 * HEAD_WIDTH
    message = (tokens // 2 + low_places(tokens, width + pair)[0], width + pair)
    anywhere = pl.BlockSpec(memory_space=pl.ANY)
    return call(
        functools.partial(low_kernel, (reach - 1, reach)),
        (shape_of((LOW_ROWS, tokens), F32), shape_of((tokens, LANES), F32))
        + (shape_of(message, BF16),) * 2,
        grid_spec=prefetch(
            1,
            (columns // tile,),
            [
                whole((tokens, width)),
                pl.BlockSpec((width, tile), lambda j, info: (0, j)),
                whole((2, tokens)),
                whole((2, tokens)),
                anywhere,
                anywhere,
            ],
            (whole((LOW_ROWS, tokens)), whole((tokens, LANES)), anywhere, anywhere),
            [
                pltpu.VMEM((2, tokens, LANES), F32),
                pltpu.VMEM((2, tokens, LANES), F32),
                pltpu.VMEM((tokens, LANES), F32),
                pltpu.VMEM((tokens, width), BF16),
                pltpu.VMEM((2, width, pair), BF16),
                pltpu.VMEM((2, *message), BF16),
                pltpu.SemaphoreType.DMA((3,)),
                pltpu.SemaphoreType.DMA((2, 2)),
            ],
        ),
    )(info, packed, weight, index.T, mix.T, x, kv_weight)


def delta_kernel(
    model_width, slots, info_ref, low_ref, opposite_ref, cw_ref, ccw_ref, total_a_ref, total_b_ref,
    weight_ref, side_ref, w_ref, out_a_ref, out_b_ref, inv_ref, co_ref, group_ref, ends, x_buf,
    w_buf, sems,
):
    step = pl.program_id(0)
    tile = w_ref.shape[0]
    half, width = x_buf.shape[1:]
    outs = (out_a_ref, out_b_ref)
    messages = (cw_ref, ccw_ref)
    end_copies = [
        pltpu.make_async_copy(ref.at[pl.ds(half, ends.shape[1])], ends.at[i], sems.at[i])
        for i, ref in enumerate(messages)
    ]
    total_copies = [
        pltpu.make_async_copy(ref, outs[i], sems.at[2 + i])
        for i, ref in enumerate((total_a_ref, total_b_ref))
    ]
    row_copies = [
        pltpu.make_async_copy(
            ref.at[pl.ds(0, half), pl.ds(0, width)], x_buf.at[i], sems.at[4 + i]
        )
        for i, ref in enumerate(messages)
    ]
    weight_copies = []
    for i in range(2):
        first = pl.multiple_of(info_ref[0, slots[i]] * width, width)
        block = weight_ref.at[pl.ds(first, width)]
        weight_copies.append(pltpu.make_async_copy(block, w_buf.at[i], sems.at[6 + i]))

    @pl.when(step == 0)
    def _():
        for copy in end_copies + total_copies + row_copies + weight_copies:
            copy.start()
        for k in range(2):
            group_ref[k] = chosen_group(side_ref[:, SIDE_INDEX + k : SIDE_INDEX + k + 1])
        for copy in end_copies:
            copy.wait()
        tokens = low_ref.shape[1]
        sums = low_ref[...] + opposite_ref[...]
        for i in range(2):
            sums = sums + read_low(ends[i].astype(F32))
        padding = jnp.zeros((LANES - LOW_ROWS, tokens), F32)
        low = jnp.concatenate([sums, padding], axis=0).T
        lane = lax.broadcasted_iota(jnp.int32, (tokens, LANES), 1)
        squares = low[:, 2 * ADAPTER_RANK : 2 * ADAPTER_RANK + 1]
        inverse = lax.rsqrt(squares * (1.0 / model_width) + EPS)
        inv_ref[...] = jnp.broadcast_to(inverse, (tokens, LANES))
        for k in range(2):
            value = fold(jnp.where(lane // ADAPTER_RANK == k, low, 0.0))
            co_ref[k] = value * inverse * side_ref[:, SIDE_MIX + k : SIDE_MIX + k + 1]
        for i in range(2):
            total_copies[i].wait()
            outs[i][...] = outs[i][...] * inverse[i * half : (i + 1) * half]

    pieces = []
    for s in range(tile // LANES):
        group = ((step * tile + s * LANES) // ADAPTER_RANK).astype(F32)
        piece = jnp.where(group_ref[0] == group, co_ref[0], 0.0)
        piece = jnp.where(group_ref[1] == group, co_ref[1], piece)
        pieces.append(piece.astype(BF16))
    coefficients = jnp.concatenate(pieces, axis=1)
    product = jnp.dot(coefficients, w_ref[...], preferred_element_type=F32)
    for i in range(2):
        outs[i][...] += product[i * half : (i + 1) * half]

    @pl.when(step == pl.num_programs(0) - 1)
    def _():
        for i in range(2):
            row_copies[i].wait()
            weight_copies[i].wait()
            product = jnp.dot(x_buf[i], w_buf[i], preferred_element_type=F32)
            out_b_ref[...] += product * inv_ref[half:, 0:1]


def query_delta(info, low, opposite, messages, slots, totals, weight, side, up):
    depth, columns = up.shape
    tile = min(DELTA_TILE, depth)
    tokens = side.shape[0]
    half = tokens // 2
    full = messages[0].shape[1]
    width = weight.shape[0] // info.shape[1]
    anywhere = pl.BlockSpec(memory_space=pl.ANY)
    extra = low_places(tokens, full)[0]
    return call(
        functools.partial(delta_kernel, weight.shape[0], slots),
        (shape_of((half, columns), F32),) * 2 + (shape_of((tokens, LANES), F32),),
        QUERY_WEIGHT,
        grid_spec=prefetch(
            1,
            (depth // tile,),
            [whole(low.shape), whole(low.shape)]
            + [anywhere] * 5
            + [whole(side.shape), pl.BlockSpec((tile, columns), lambda j, _: (j, 0))],
            (whole((half, columns)), whole((half, columns)), whole((tokens, LANES))),
            [
                pltpu.VMEM((2, tokens, LANES), F32),
                pltpu.VMEM((2, tokens, LANES), F32),
                pltpu.VMEM((2, extra, full), BF16),
                pltpu.VMEM((2, half, width), BF16),
                pltpu.VMEM((2, width, columns), BF16),
                pltpu.SemaphoreType.DMA((8,)),
            ],
        ),
    )(info, low, opposite, *messages, *totals, weight, side, up)


def product_kernel(slots, starts, has_total, has_inv, info_ref, *refs):
    refs = list(refs)
    count = len(slots)
    blocks = [refs.pop(0) for _ in range(count)]
    weight = refs.pop(0)
    total_ref = refs.pop(0) if has_total else None
    inv_ref = refs.pop(0) if has_inv else None
    out_ref, x_buf, w_buf, sems, total_sem = refs
    depth, half, width = x_buf.shape
    columns = w_buf.shape[2]
    chunk = min(CHUNK, columns)

    def copies(i):
        buf = i % depth
        first = pl.multiple_of(info_ref[0, slots[i]] * width, width)
        block = blocks[i].at[pl.ds(starts[i], half), pl.ds(0, width)]
        return [
            pltpu.make_async_copy(weight.at[pl.ds(first, width)], w_buf.at[buf], sems.at[buf, 0]),
            pltpu.make_async_copy(block, x_buf.at[buf], sems.at[buf, 1]),
        ]

    for i in range(min(depth - 1, count)):
        for copy in copies(i):
            copy.start()
    if has_total:
        total_copy = pltpu.make_async_copy(total_ref, out_ref, total_sem)
        total_copy.start()
    for i in range(count):
        buf = i % depth
        if i + depth - 1 < count:
            for copy in copies(i + depth - 1):
                copy.start()
        for copy in copies(i):
            copy.wait()
        if i == 0 and has_total:
            total_copy.wait()
        for first in range(0, columns, chunk):
            span = slice(first, first + chunk)
            value = jnp.dot(x_buf[buf], w_buf[buf, :, span], preferred_element_type=F32)
            if has_inv:
                value = value * inv_ref[:, 0:1]
            if i > 0 or has_total:
                value = out_ref[:, span] + value
            out_ref[:, span] = value


def product(info, total, sources, weight, half, inv=None, place=0):
    columns = weight.shape[1]
    width = weight.shape[0] // info.shape[1]
    operands = [block for _, block, _ in sources] + [weight] + ([] if total is None else [total])
    in_specs = [pl.BlockSpec(memory_space=pl.ANY)] * len(operands)
    if inv is not None:
        operands.append(inv)
        in_specs.append(pl.BlockSpec((half, LANES), lambda j, info: (place, 0)))
    slots = [slot for slot, _, _ in sources]
    starts = [start for _, _, start in sources]
    return call(
        functools.partial(product_kernel, slots, starts, total is not None, inv is not None),
        shape_of((half, columns), F32),
        QUERY_WEIGHT,
        grid_spec=prefetch(
            1,
            (1,),
            in_specs,
            whole((half, columns)),
            [
                pltpu.VMEM((DEPTH, half, width), BF16),
                pltpu.VMEM((DEPTH, width, columns), BF16),
                pltpu.SemaphoreType.DMA((DEPTH, 2)),
                pltpu.SemaphoreType.DMA,
            ],
        ),
    )(info, *operands)


def rotate(values, cosines, sines):
    lane = lax.broadcasted_iota(jnp.int32, values.shape, 1)
    other = jnp.take_along_axis(values, lane ^ 1, axis=1, mode="promise_in_bounds")
    return values * cosines + other * sines


def attention_kernel(
    info_ref, lengths_ref, total_a_ref, total_b_ref, inv_ref, w_ref, cos_ref, sin_ref, own_ref,
    *refs,
):
    parts, sums = refs[:4], refs[4:10]
    out_ref, last_s, key_s, value_s, bias_s = refs[10:]
    mid = parts[0].shape[0]

    @pl.when(pl.program_id(0) == 0)
    def _():
        row = lax.broadcasted_iota(jnp.int32, (SLOT, SLOT), 0)
        col = lax.broadcasted_iota(jnp.int32, (SLOT, SLOT), 1)
        for i, part in enumerate(parts):
            last_s[i * mid : (i + 1) * mid, :] = part[...]
        for prompt in range(2):
            span = slice(prompt * SLOT, (prompt + 1) * SLOT)
            first, second, other = sums[3 * prompt : 3 * prompt + 3]
            pair = jnp.concatenate([first[...], second[...]], axis=0).astype(F32)
            pair = pair + other[...].astype(F32) + own_ref[span, :].astype(F32)
            pair = pair * inv_ref[span, 0:1]
            key = rotate(pair[:, :HEAD_WIDTH], cos_ref[...], sin_ref[...])
            key_s[prompt] = key.astype(BF16)
            value_s[prompt, :, :HEAD_WIDTH] = pair[:, HEAD_WIDTH:].astype(BF16)
            value_s[prompt, :, HEAD_WIDTH:] = jnp.ones((SLOT, HEAD_WIDTH), BF16)
            seen = (col <= row) & (col < lengths_ref[prompt])
            bias_s[prompt] = jnp.where(seen, 0.0, -1e30)

    product = jnp.dot(last_s[...], w_ref[...], preferred_element_type=F32)
    row_narrow = lax.broadcasted_iota(jnp.int32, (SLOT, HEAD_WIDTH), 0)
    factor = math.log2(math.e) / math.sqrt(HEAD_WIDTH)
    for prompt, total_ref in enumerate((total_a_ref, total_b_ref)):
        rows = slice(prompt * SLOT, (prompt + 1) * SLOT)
        queries = total_ref[...] + product[rows] * inv_ref[rows, 0:1]
        for head in range(w_ref.shape[1] // HEAD_WIDTH):
            span = slice(head * HEAD_WIDTH, (head + 1) * HEAD_WIDTH)
            query = rotate(queries[:, span], cos_ref[...], sin_ref[...]).astype(BF16)
            scores = lax.dot_general(
                query, key_s[prompt], (((1,), (1,)), ((), ())), preferred_element_type=F32
            )
            scores = scores * factor + bias_s[prompt]
            top = jnp.max(scores, axis=1, keepdims=True)
            weights = jnp.exp2(scores - top)
            mixed = jnp.dot(weights.astype(BF16), value_s[prompt], preferred_element_type=F32)
            mixed = mixed[:, :HEAD_WIDTH] / mixed[:, HEAD_WIDTH:]
            mixed = jnp.where(row_narrow < lengths_ref[prompt], mixed, 0.0)
            out_ref[rows, span] = mixed.astype(BF16)


def attention(info, lengths, totals, inv, last_slot, weight, own, parts, tables):
    width = weight.shape[0] // info.shape[1]
    columns = weight.shape[1]
    tile = min(HEADS_AT_ONCE * HEAD_WIDTH, columns)
    pair = 2 * HEAD_WIDTH
    mid = SLOT // 2
    tokens = 2 * SLOT
    rows_of = [part for first, second, _ in parts for part in (first, second)]
    sums_of = [part for first, _, other in parts for part in (first, first, other)]
    lane = width // pair
    sums_specs = [
        pl.BlockSpec((mid, pair), lambda j, *_: (0, lane)),
        pl.BlockSpec((mid, pair), lambda j, *_: (0, lane + 1)),
        pl.BlockSpec((SLOT, pair), lambda j, *_: (0, lane)),
    ]
    return call(
        attention_kernel,
        shape_of((tokens, columns), BF16),
        grid_spec=prefetch(
            2,
            (columns // tile,),
            [
                pl.BlockSpec((SLOT, tile), lambda j, *_: (0, j)),
                pl.BlockSpec((SLOT, tile), lambda j, *_: (0, j)),
                whole((tokens, LANES)),
                pl.BlockSpec((width, tile), lambda j, info, _: (info[0, last_slot], j)),
                whole((SLOT, HEAD_WIDTH)),
                whole((SLOT, HEAD_WIDTH)),
                whole((tokens, pair)),
            ]
            + [pl.BlockSpec((mid, width), lambda j, *_: (0, 0))] * 4
            + sums_specs * 2,
            pl.BlockSpec((tokens, tile), lambda j, *_: (0, j)),
            [
                pltpu.VMEM((tokens, width), BF16),
                pltpu.VMEM((2, SLOT, HEAD_WIDTH), BF16),
                pltpu.VMEM((2, SLOT, 2 * HEAD_WIDTH), BF16),
                pltpu.VMEM((2, SLOT, SLOT), F32),
            ],
        ),
    )(info, lengths, *totals, inv, weight, *tables, own, *rows_of, *sums_of)


def rotation_tables():
    lane = jnp.arange(HEAD_WIDTH)
    inverse = jnp.power(F32(ROPE_BASE), -2.0 * (lane // 2).astype(F32) / HEAD_WIDTH)
    angles = jnp.arange(SLOT).astype(F32)[:, None] * inverse[None, :]
    sines = jnp.sin(angles)
    return jnp.cos(angles), jnp.where(lane[None, :] % 2 == 0, -sines, sines)


def ring_order(count):
    if count > 8:
        return list(range(count))
    return list(range(0, count, 2)) + list(range(1, count, 2))[::-1]


def after(value, *earlier):
    return lax.optimization_barrier((value, *earlier))[0]


def program(count, rows, lengths, info, x, scale, wq, wkv, wdown, wup, index, mix):
    order = ring_order(count)
    reach = count // 2
    cw = [(order[i], order[(i + 1) % count]) for i in range(count)]
    ccw = [(b, a) for a, b in cw]
    send_cw = functools.partial(lax.ppermute, axis_name="tensor", perm=cw)
    send_ccw = functools.partial(lax.ppermute, axis_name="tensor", perm=ccw)

    opposite = [(order[i], order[(i + reach) % count]) for i in range(count)]

    cw_first, ccw_first, packed = scale_rows(info, x, scale, wkv, reach)
    from_cw, from_ccw = [send_cw(cw_first), None], [send_ccw(ccw_first), None]
    low, side, cw_second, ccw_second = low_partials(
        info, x, packed, wdown, index, mix, wkv, reach
    )
    from_cw[1], from_ccw[1] = send_cw(cw_second), send_ccw(ccw_second)
    done = low
    totals = [None, None]
    inv = None
    last = []
    terms = None
    half = rows // 2

    for step in range(1, reach):
        final = step + 1 == reach
        for piece in range(2):
            got_cw, got_ccw, _ = lax.optimization_barrier((from_cw[piece], from_ccw[piece], done))
            aways = [reach - step - piece, count - reach + step + 1 - piece]
            ends = got_cw, got_ccw
            moved = list(ends)
            if final:
                sums_from, other = ends if piece == 0 else ends[::-1]
                first, second = last_messages(
                    info, sums_from, other, aways[piece], packed, wkv, terms, rows, piece
                )
                if piece == 0:
                    last.append((send_cw(first), send_ccw(second), got_ccw))
                else:
                    last.append((send_ccw(first), send_cw(second), got_cw))
                done = first
            else:
                if piece == 0:
                    moved = add_terms(info, moved, aways, packed, wkv, terms, rows)
                else:
                    moved = add_terms_low(
                        info, moved, aways, packed, wkv, terms, low, rows, step < reach - 2
                    )
                from_cw[piece], from_ccw[piece] = send_cw(moved[0]), send_ccw(moved[1])
                done = moved[piece]
            sources = [(count - step, moved[0], 0), (step, moved[1], 0)]
            if step == 1:
                sources = [(0, packed, piece * half)] + sources
            if step == 1 and piece == 1:
                opposite_low = lax.ppermute(moved[2], "tensor", opposite)
            if step == reach - 2 and piece == 1:
                late, _ = lax.optimization_barrier((opposite_low, done))
                *totals, inv = query_delta(
                    info, low, late, ends, (count - step, step), totals, wq, side, wup
                )
                done = inv
            else:
                totals[piece] = product(info, totals[piece], sources, wq, half, inv, piece)
                done = totals[piece]
            if step == 1 and piece == 0:
                *late, own = late_terms(info, after(packed, done), wkv, count)
                done = late[0]
            if step == 1 and piece == 1:
                terms = late
    return attention(info, lengths, totals, inv, reach, wq, own, last, rotation_tables())


def shards(count, x, scale, wq, wkv, wdown, wup, index, mix, lengths):
    shard = lax.axis_index("tensor")
    order = ring_order(count)
    heads = wq.shape[1] // HEAD_WIDTH
    table = np.zeros((count, 2, count), np.int32)
    for place, device in enumerate(order):
        for i in range(count):
            other = order[(place + i) % count]
            table[device, 0, i] = other
            table[device, 1, i] = other * heads // (QUERY_HEADS // KV_HEADS)
    info = lax.dynamic_index_in_dim(jnp.asarray(table), shard, 0, keepdims=False)
    return program(count, x.shape[0], lengths, info, x, scale, wq, wkv, wdown, wup, index, mix)


def solution(mesh):
    placed = (
        P(("groups", "replica"), "tensor"),
        P(),
        P(None, "tensor"),
        P("tensor", None),
        P("tensor", None),
        P(None, "tensor"),
        P(("groups", "replica"), None),
        P(("groups", "replica"), None),
        P(("groups", "replica")),
    )
    return jax.shard_map(
        functools.partial(shards, mesh.shape["tensor"]),
        mesh=mesh,
        in_specs=placed,
        out_specs=P(("groups", "replica"), "tensor"),
        check_vma=False,
    )
```

```python
import functools
import math

import jax
import jax.numpy as jnp
import numpy as np
from jax import lax
from jax.experimental import pallas as pl
from jax.experimental.pallas import tpu as pltpu
from jax.sharding import PartitionSpec as P

QUERY_HEADS = 64
KV_HEADS = 8
HEAD_WIDTH = 128
ADAPTER_RANK = 16
SLOT = 256
LANES = 128
LOW_ROWS = 40

EPS = 1e-05
ROPE_BASE = 500000.0

SIDE_MIX = 0
SIDE_INDEX = 2

DEPTH = 3
CHUNK = 512
HEADS_AT_ONCE = 8
DELTA_TILE = 1024
ADD_WEIGHT = 8.0
QUERY_WEIGHT = 8.0
VMEM_LIMIT = 64 * 1024 * 1024 - 64 * 1024
F32 = jnp.float32
BF16 = jnp.bfloat16


def call(kernel, out_shape, microseconds=0.0, **kwargs):
    return pl.pallas_call(
        kernel,
        out_shape=out_shape,
        compiler_params=pltpu.CompilerParams(vmem_limit_bytes=VMEM_LIMIT),
        cost_estimate=pl.CostEstimate(
            flops=int(1.15e9 * microseconds), bytes_accessed=1000, transcendentals=0
        ),
        **kwargs,
    )


def whole(shape):
    return pl.BlockSpec(shape, lambda *_: (0,) * len(shape))


def shape_of(shape, dtype):
    return jax.ShapeDtypeStruct(shape, dtype)


def prefetch(count, grid, in_specs, out_specs, scratch_shapes=()):
    return pltpu.PrefetchScalarGridSpec(
        num_scalar_prefetch=count,
        grid=grid,
        in_specs=in_specs,
        out_specs=out_specs,
        scratch_shapes=scratch_shapes,
    )


def write_message(message, block, w_ref):
    half, width = block.shape
    message[:half, :width] = block
    product = jnp.dot(block, w_ref[...], preferred_element_type=F32)
    message[:half, width:] = product.astype(BF16)


def scale_kernel(info_ref, x_ref, scale_ref, cw_w_ref, ccw_w_ref, cw_ref, ccw_ref, packed):
    half = cw_ref.shape[0]
    packed[...] = (x_ref[...].astype(F32) * scale_ref[...]).astype(BF16)
    block = packed[:half, :]
    write_message(cw_ref, block, cw_w_ref)
    write_message(ccw_ref, block, ccw_w_ref)


def scale_rows(info, x, scale, weight, reach):
    tokens, width = x.shape
    pair = 2 * HEAD_WIDTH
    message = (tokens // 2, width + pair)
    column = [
        pl.BlockSpec((width, pair), lambda j, info, away=away: (0, info[1, away]))
        for away in (reach, reach + 1)
    ]
    return call(
        scale_kernel,
        (shape_of(message, BF16),) * 2 + (shape_of((tokens, width), BF16),),
        grid_spec=prefetch(
            1,
            (1,),
            [
                whole((tokens, width)),
                pl.BlockSpec((1, width), lambda j, info: (0, info[0, 0])),
                *column,
            ],
            (whole(message),) * 2 + (whole((tokens, width)),),
        ),
    )(info, x, scale.reshape(1, -1), weight, weight)


def low_places(tokens, full):
    if full >= 2 * tokens + SLOT:
        second = (slice(0, ADAPTER_RANK), slice(tokens, 2 * tokens))
        squares = (0, slice(2 * tokens, 2 * tokens + SLOT))
        extra = ADAPTER_RANK
    else:
        second = (slice(ADAPTER_RANK, 2 * ADAPTER_RANK), slice(0, tokens))
        squares = (2 * ADAPTER_RANK, slice(0, SLOT))
        extra = 3 * ADAPTER_RANK
    return extra, (slice(0, ADAPTER_RANK), slice(0, tokens)), second, squares


def read_low(region):
    tokens = 2 * SLOT
    _, first, second, (row, lanes) = low_places(tokens, region.shape[1])
    squares = jnp.concatenate(
        [region[row + i : row + i + 1, lanes] + region[row + 2 + i : row + 3 + i, lanes] for i in range(2)],
        axis=1,
    )
    return jnp.concatenate(
        [region[first], region[second], squares, jnp.zeros((LOW_ROWS - 33, tokens), F32)], axis=0
    )


def write_low(message, half, low):
    tokens = 2 * SLOT
    extra, first, second, (row, lanes) = low_places(tokens, message.shape[1])
    message[half : half + extra, :] = jnp.zeros((extra, message.shape[1]), BF16)
    squares = low[2 * ADAPTER_RANK : 2 * ADAPTER_RANK + 1, :]
    rounded = squares.astype(BF16)
    rest = (squares - rounded.astype(F32)).astype(BF16)
    for place, value in ((first, low[:ADAPTER_RANK]), (second, low[ADAPTER_RANK : 2 * ADAPTER_RANK])):
        span = slice(half + place[0].start, half + place[0].stop)
        message[span, place[1]] = value.astype(BF16)
    block = jnp.concatenate(
        [rounded[:, :SLOT], rounded[:, SLOT:], rest[:, :SLOT], rest[:, SLOT:]]
        + [jnp.zeros((ADAPTER_RANK - 4, SLOT), BF16)],
        axis=0,
    )
    message[half + row : half + row + ADAPTER_RANK, lanes] = block


def terms_kernel(
    info_ref, x_ref, ahead_w_ref, behind_w_ref, own_w_ref, ahead_ref, behind_ref, own_ref
):
    @pl.when(pl.program_id(0) == 0)
    def _():
        own = jnp.dot(x_ref[...], own_w_ref[...], preferred_element_type=F32)
        own_ref[...] = own.astype(BF16)

    for w_ref, out_ref in ((ahead_w_ref, ahead_ref), (behind_w_ref, behind_ref)):
        out_ref[0] = jnp.dot(x_ref[...], w_ref[...], preferred_element_type=F32).astype(BF16)


def late_terms(info, packed, weight, count):
    rows, width = packed.shape
    pair = 2 * HEAD_WIDTH
    number = count // 2 - 2
    out = shape_of((number, rows, pair), BF16)
    block = pl.BlockSpec((1, rows, pair), lambda i, info: (i, 0, 0))
    return call(
        terms_kernel,
        (out, out, shape_of((rows, pair), BF16)),
        grid_spec=prefetch(
            1,
            (number,),
            [
                whole((rows, width)),
                pl.BlockSpec((width, pair), lambda i, info: (0, info[1, 1 + i])),
                pl.BlockSpec((width, pair), lambda i, info: (0, info[1, count - 1 - i])),
                pl.BlockSpec((width, pair), lambda i, info: (0, info[1, 0])),
            ],
            (block, block, whole((rows, pair))),
        ),
    )(info, packed, weight, weight, weight)


def own_term(block_ref, w_ref):
    if block_ref is None:
        return w_ref[0].astype(F32)
    return jnp.dot(block_ref[...], w_ref[...], preferred_element_type=F32)


def term_specs(info, aways, packed, weight, terms, piece):
    rows, width = packed.shape
    half = rows // 2
    pair = 2 * HEAD_WIDTH
    if terms is None:
        specs = [pl.BlockSpec((half, width), lambda j, info: (piece, 0))]
        specs += [
            pl.BlockSpec((width, pair), lambda j, info, away=away: (0, info[1, away]))
            for away in aways
        ]
        return [packed] + [weight] * len(aways), specs
    count = info.shape[1]
    operands, specs = [], []
    for away in aways:
        ahead = away < count // 2
        operands.append(terms[0 if ahead else 1])
        place = away - 1 if ahead else count - 1 - away
        specs.append(pl.BlockSpec((1, half, pair), lambda j, info, place=place: (place, piece, 0)))
    return operands, specs


def add_kernel(ready, info_ref, *refs):
    refs = list(refs)
    messages = [refs.pop(0), refs.pop(0)]
    block = None if ready else refs.pop(0)
    for i, message in enumerate(messages):
        total = message[...].astype(F32) + own_term(block, refs[i])
        refs[2 + i][...] = total.astype(BF16)


def add_terms(info, messages, aways, packed, weight, terms, rows):
    half = rows // 2
    full = messages[0].shape[1]
    pair = 2 * HEAD_WIDTH
    lanes = pl.BlockSpec((half, pair), lambda j, info: (0, full // pair - 1))
    operands, specs = term_specs(info, aways, packed, weight, terms, 0)
    return call(
        functools.partial(add_kernel, terms is not None),
        (shape_of((half, full), BF16),) * 2,
        ADD_WEIGHT,
        grid_spec=prefetch(1, (1,), [lanes] * 2 + specs, (lanes,) * 2),
        input_output_aliases={1: 0, 2: 1},
    )(info, *messages, *operands)


def add_low_kernel(half, ready, info_ref, low_ref, *refs):
    refs = list(refs)
    pair = 2 * HEAD_WIDTH
    around = low_ref[...]
    messages = [refs.pop(0), refs.pop(0)]
    block = None if ready else refs.pop(0)
    for i, given in enumerate(messages):
        out = refs[2 + i]
        full = given.shape[1]
        out[:half, : full - pair] = given[:half, : full - pair]
        own = own_term(block, refs[i])
        out[:half, full - pair :] = (given[:half, full - pair :].astype(F32) + own).astype(BF16)
        if out.shape[0] > half:
            sums = read_low(given[half:, :].astype(F32))
            around = around + sums
            write_low(out, half, sums + low_ref[...])
    if len(refs) > 4:
        refs[4][...] = around


def add_terms_low(info, messages, aways, packed, weight, terms, low, rows, keep):
    half = rows // 2
    shape = messages[0].shape
    after = shape if keep else (half, shape[1])
    out = (shape_of(after, BF16),) * 2 + ((shape_of(low.shape, F32),) if keep else ())
    operands, specs = term_specs(info, aways, packed, weight, terms, 1)
    return call(
        functools.partial(add_low_kernel, half, terms is not None),
        out,
        ADD_WEIGHT,
        grid_spec=prefetch(
            1,
            (1,),
            [whole(low.shape)] + [whole(shape)] * 2 + specs,
            tuple(whole(each.shape) for each in out),
        ),
    )(info, low, *messages, *operands)


def last_shares(half, width):
    groups = width // (2 * HEAD_WIDTH)
    below = half // groups
    return groups, below, max(16, (half - below) // 2)


def last_kernel(half, ready, info_ref, with_sums, other, *refs):
    refs = list(refs)
    block = None if ready else refs.pop(0)
    term, first_ref, second_ref = refs
    width = second_ref.shape[1]
    pair = 2 * HEAD_WIDTH
    groups, below, share = last_shares(half, width)
    own = own_term(block, term)
    sums = (with_sums[:half, width:].astype(F32) + own).astype(BF16)
    first_ref[:share, :] = with_sums[:share, :width]
    for i in range(groups):
        lanes = slice(i * pair, (i + 1) * pair)
        first_ref[share:, lanes] = sums[i * below : (i + 1) * below]
    second_ref[...] = other[share:half, :width]


def last_messages(info, with_sums, other, away, packed, weight, terms, rows, piece):
    half = rows // 2
    width = weight.shape[0]
    pair = 2 * HEAD_WIDTH
    _, below, share = last_shares(half, width)
    out = (shape_of((share + below, width), BF16), shape_of((half - share, width), BF16))
    operands, specs = term_specs(info, [away], packed, weight, terms, piece)
    return call(
        functools.partial(last_kernel, half, terms is not None),
        out,
        ADD_WEIGHT,
        grid_spec=prefetch(
            1,
            (1,),
            [whole(with_sums.shape), whole(other.shape)] + specs,
            tuple(whole(each.shape) for each in out),
        ),
    )(info, with_sums, other, *operands)


def chosen_group(index):
    rows = index.shape[0]
    lane = lax.broadcasted_iota(jnp.int32, (rows, LANES), 1)
    return index - (lane // ADAPTER_RANK).astype(F32)


def fold(value):
    shift = ADAPTER_RANK
    while shift < LANES:
        value = value + pltpu.roll(value, shift, 1)
        shift *= 2
    return value


def low_kernel(
    aways, info_ref, packed_ref, w_ref, index_ref, mix_ref, x_ref, kv_ref, out_ref, side_ref,
    cw_ref, ccw_ref, acc_ref, group_ref, squares_ref, x_s, columns_s, messages_s, sems,
    out_sems,
):
    step = pl.program_id(0)
    tile = w_ref.shape[1]
    tokens = x_ref.shape[0]
    half = tokens // 2
    pair = 2 * HEAD_WIDTH
    reads = [pltpu.make_async_copy(x_ref, x_s, sems.at[0])]
    for i, away in enumerate(aways):
        first = pl.multiple_of(info_ref[1, away] * pair, pair)
        column = kv_ref.at[:, pl.ds(first, pair)]
        reads.append(pltpu.make_async_copy(column, columns_s.at[i], sems.at[1 + i]))
    writes = []
    for i, ref in enumerate((cw_ref, ccw_ref)):
        extra = ref.shape[0] - half
        for j, span in enumerate((pl.ds(0, half), pl.ds(half, extra))):
            block = messages_s.at[i, span]
            writes.append(pltpu.make_async_copy(block, ref.at[span], out_sems.at[i, j]))

    @pl.when(step == 0)
    def _():
        for copy in reads:
            copy.start()
        acc_ref[...] = jnp.zeros_like(acc_ref)
        side = jnp.concatenate(
            [mix_ref[...], index_ref[...].astype(F32), jnp.zeros((LANES - 4, tokens), F32)],
            axis=0,
        ).T
        side_ref[...] = side
        for k in range(2):
            group_ref[k] = chosen_group(side[:, SIDE_INDEX + k : SIDE_INDEX + k + 1])

    @pl.when(step == 1)
    def _():
        for copy in reads:
            copy.wait()
        x = x_s[...].astype(F32)
        squares = jnp.sum(x * x, axis=1, keepdims=True)
        squares_ref[...] = jnp.broadcast_to(squares, squares_ref.shape)
        for i in range(2):
            write_message(messages_s.at[i], packed_ref[half:, :], columns_s.at[i])
            writes[2 * i].start()
    chunk = min(CHUNK, tile)
    for first in range(0, tile, chunk):
        product = jnp.dot(
            packed_ref[...], w_ref[:, first : first + chunk], preferred_element_type=F32
        )
        for k in range(2):
            total = acc_ref[k]
            for s in range(chunk // LANES):
                group = (step * tile + first + s * LANES) // ADAPTER_RANK
                here = group_ref[k] == group.astype(F32)
                total += jnp.where(here, product[:, s * LANES : (s + 1) * LANES], 0.0)
            acc_ref[k] = total

    @pl.when(step == pl.num_programs(0) - 1)
    def _():
        lane = lax.broadcasted_iota(jnp.int32, (tokens, LANES), 1)
        sums = jnp.where(lane < ADAPTER_RANK, fold(acc_ref[0]), fold(acc_ref[1]))
        sums = jnp.where(lane < 2 * ADAPTER_RANK, sums, 0.0)
        sums = jnp.where(lane == 2 * ADAPTER_RANK, squares_ref[...], sums)
        low = sums.T[:LOW_ROWS]
        out_ref[...] = low
        for i in range(2):
            write_low(messages_s.at[i], half, low)
            writes[2 * i + 1].start()
        for copy in writes:
            copy.wait()


def low_partials(info, x, packed, weight, index, mix, kv_weight, reach):
    width, columns = weight.shape
    tile = min(1024, columns)
    tokens = x.shape[0]
    pair = 2 * HEAD_WIDTH
    message = (tokens // 2 + low_places(tokens, width + pair)[0], width + pair)
    anywhere = pl.BlockSpec(memory_space=pl.ANY)
    return call(
        functools.partial(low_kernel, (reach - 1, reach)),
        (shape_of((LOW_ROWS, tokens), F32), shape_of((tokens, LANES), F32))
        + (shape_of(message, BF16),) * 2,
        grid_spec=prefetch(
            1,
            (columns // tile,),
            [
                whole((tokens, width)),
                pl.BlockSpec((width, tile), lambda j, info: (0, j)),
                whole((2, tokens)),
                whole((2, tokens)),
                anywhere,
                anywhere,
            ],
            (whole((LOW_ROWS, tokens)), whole((tokens, LANES)), anywhere, anywhere),
            [
                pltpu.VMEM((2, tokens, LANES), F32),
                pltpu.VMEM((2, tokens, LANES), F32),
                pltpu.VMEM((tokens, LANES), F32),
                pltpu.VMEM((tokens, width), BF16),
                pltpu.VMEM((2, width, pair), BF16),
                pltpu.VMEM((2, *message), BF16),
                pltpu.SemaphoreType.DMA((3,)),
                pltpu.SemaphoreType.DMA((2, 2)),
            ],
        ),
    )(info, packed, weight, index.T, mix.T, x, kv_weight)


def delta_kernel(
    model_width, slots, info_ref, low_ref, opposite_ref, cw_ref, ccw_ref, total_a_ref, total_b_ref,
    weight_ref, side_ref, w_ref, out_a_ref, out_b_ref, inv_ref, co_ref, group_ref, ends, x_buf,
    w_buf, total_buf, sems,
):
    step = pl.program_id(0)
    tile = w_ref.shape[0]
    half, width = x_buf.shape[1:]
    outs = (out_a_ref, out_b_ref)
    messages = (cw_ref, ccw_ref)
    end_copies = [
        pltpu.make_async_copy(ref.at[pl.ds(half, ends.shape[1])], ends.at[i], sems.at[i])
        for i, ref in enumerate(messages)
    ]
    total_copies = [
        pltpu.make_async_copy(ref, total_buf.at[i], sems.at[2 + i])
        for i, ref in enumerate((total_a_ref, total_b_ref))
    ]
    row_copies = [
        pltpu.make_async_copy(
            ref.at[pl.ds(0, half), pl.ds(0, width)], x_buf.at[i], sems.at[4 + i]
        )
        for i, ref in enumerate(messages)
    ]
    weight_copies = []
    for i in range(2):
        first = pl.multiple_of(info_ref[0, slots[i]] * width, width)
        block = weight_ref.at[pl.ds(first, width)]
        weight_copies.append(pltpu.make_async_copy(block, w_buf.at[i], sems.at[6 + i]))

    @pl.when(step == 0)
    def _():
        for copy in end_copies:
            copy.start()
        for k in range(2):
            group_ref[k] = chosen_group(side_ref[:, SIDE_INDEX + k : SIDE_INDEX + k + 1])
        for copy in end_copies:
            copy.wait()
        tokens = low_ref.shape[1]
        sums = low_ref[...] + opposite_ref[...]
        for i in range(2):
            sums = sums + read_low(ends[i].astype(F32))
        padding = jnp.zeros((LANES - LOW_ROWS, tokens), F32)
        low = jnp.concatenate([sums, padding], axis=0).T
        lane = lax.broadcasted_iota(jnp.int32, (tokens, LANES), 1)
        squares = low[:, 2 * ADAPTER_RANK : 2 * ADAPTER_RANK + 1]
        inverse = lax.rsqrt(squares * (1.0 / model_width) + EPS)
        inv_ref[...] = jnp.broadcast_to(inverse, (tokens, LANES))
        for k in range(2):
            value = fold(jnp.where(lane // ADAPTER_RANK == k, low, 0.0))
            co_ref[k] = value * inverse * side_ref[:, SIDE_MIX + k : SIDE_MIX + k + 1]
        for i in range(2):
            outs[i][...] = jnp.zeros_like(outs[i])
        for copy in total_copies + row_copies + weight_copies:
            copy.start()

    pieces = []
    for s in range(tile // LANES):
        group = ((step * tile + s * LANES) // ADAPTER_RANK).astype(F32)
        piece = jnp.where(group_ref[0] == group, co_ref[0], 0.0)
        piece = jnp.where(group_ref[1] == group, co_ref[1], piece)
        pieces.append(piece.astype(BF16))
    coefficients = jnp.concatenate(pieces, axis=1)
    product = jnp.dot(coefficients, w_ref[...], preferred_element_type=F32)
    for i in range(2):
        outs[i][...] += product[i * half : (i + 1) * half]

    @pl.when(step == pl.num_programs(0) - 1)
    def _():
        for copy in total_copies + row_copies + weight_copies:
            copy.wait()
        out_a_ref[...] += total_buf[0] * inv_ref[:half, 0:1]
        total = total_buf[1]
        for i in range(2):
            total += jnp.dot(x_buf[i], w_buf[i], preferred_element_type=F32)
        out_b_ref[...] += total * inv_ref[half:, 0:1]


def query_delta(info, low, opposite, messages, slots, totals, weight, side, up):
    depth, columns = up.shape
    tile = min(DELTA_TILE, depth)
    tokens = side.shape[0]
    half = tokens // 2
    full = messages[0].shape[1]
    width = weight.shape[0] // info.shape[1]
    anywhere = pl.BlockSpec(memory_space=pl.ANY)
    extra = low_places(tokens, full)[0]
    return call(
        functools.partial(delta_kernel, weight.shape[0], slots),
        (shape_of((half, columns), F32),) * 2 + (shape_of((tokens, LANES), F32),),
        QUERY_WEIGHT,
        grid_spec=prefetch(
            1,
            (depth // tile,),
            [whole(low.shape), whole(low.shape)]
            + [anywhere] * 5
            + [whole(side.shape), pl.BlockSpec((tile, columns), lambda j, _: (j, 0))],
            (whole((half, columns)), whole((half, columns)), whole((tokens, LANES))),
            [
                pltpu.VMEM((2, tokens, LANES), F32),
                pltpu.VMEM((2, tokens, LANES), F32),
                pltpu.VMEM((2, extra, full), BF16),
                pltpu.VMEM((2, half, width), BF16),
                pltpu.VMEM((2, width, columns), BF16),
                pltpu.VMEM((2, half, columns), F32),
                pltpu.SemaphoreType.DMA((8,)),
            ],
        ),
    )(info, low, opposite, *messages, *totals, weight, side, up)


def product_kernel(slots, starts, has_total, has_inv, place, info_ref, *refs):
    refs = list(refs)
    count = len(slots)
    blocks = [refs.pop(0) for _ in range(count)]
    weight = refs.pop(0)
    late = [refs.pop(0) for _ in range(has_total + has_inv)]
    out_ref, x_buf, w_buf, sems, late_sems, *late_bufs = refs
    depth, half, width = x_buf.shape
    columns = w_buf.shape[2]
    chunk = min(CHUNK, columns)

    def copies(i):
        buf = i % depth
        first = pl.multiple_of(info_ref[0, slots[i]] * width, width)
        block = blocks[i].at[pl.ds(starts[i], half), pl.ds(0, width)]
        return [
            pltpu.make_async_copy(weight.at[pl.ds(first, width)], w_buf.at[buf], sems.at[buf, 0]),
            pltpu.make_async_copy(block, x_buf.at[buf], sems.at[buf, 1]),
        ]

    for i in range(min(depth - 1, count)):
        for copy in copies(i):
            copy.start()
    if has_inv:
        late[-1] = late[-1].at[pl.ds(place * half, half)]
    late_copies = [
        pltpu.make_async_copy(ref, late_bufs[i], late_sems.at[i]) for i, ref in enumerate(late)
    ]
    for copy in late_copies:
        copy.start()
    for i in range(count):
        buf = i % depth
        if i + depth - 1 < count:
            for copy in copies(i + depth - 1):
                copy.start()
        for copy in copies(i):
            copy.wait()
        if i == count - 1:
            for copy in late_copies:
                copy.wait()
        for first in range(0, columns, chunk):
            span = slice(first, first + chunk)
            value = jnp.dot(x_buf[buf], w_buf[buf, :, span], preferred_element_type=F32)
            if i > 0:
                value = out_ref[:, span] + value
            if i == count - 1 and has_inv:
                value = value * late_bufs[-1][:, 0:1]
            if i == count - 1 and has_total:
                value = late_bufs[0][:, span] + value
            out_ref[:, span] = value


def product(info, total, sources, weight, half, inv=None, place=0):
    columns = weight.shape[1]
    width = weight.shape[0] // info.shape[1]
    operands = [block for _, block, _ in sources] + [weight]
    late = []
    if total is not None:
        operands.append(total)
        late.append(pltpu.VMEM((half, columns), F32))
    if inv is not None:
        operands.append(inv)
        late.append(pltpu.VMEM((half, LANES), F32))
    in_specs = [pl.BlockSpec(memory_space=pl.ANY)] * len(operands)
    slots = [slot for slot, _, _ in sources]
    starts = [start for _, _, start in sources]
    return call(
        functools.partial(
            product_kernel, slots, starts, total is not None, inv is not None, place
        ),
        shape_of((half, columns), F32),
        QUERY_WEIGHT,
        grid_spec=prefetch(
            1,
            (1,),
            in_specs,
            whole((half, columns)),
            [
                pltpu.VMEM((DEPTH, half, width), BF16),
                pltpu.VMEM((DEPTH, width, columns), BF16),
                pltpu.SemaphoreType.DMA((DEPTH, 2)),
                pltpu.SemaphoreType.DMA((2,)),
                *late,
            ],
        ),
    )(info, *operands)


def rotate(values, cosines, sines):
    lane = lax.broadcasted_iota(jnp.int32, values.shape, 1)
    other = jnp.take_along_axis(values, lane ^ 1, axis=1, mode="promise_in_bounds")
    return values * cosines + other * sines


def attention_kernel(
    info_ref, lengths_ref, total_a_ref, total_b_ref, inv_ref, w_ref, cos_ref, sin_ref, own_ref,
    *refs,
):
    parts, others = refs[:4], refs[4:6]
    out_ref, last_s, key_s, value_s, bias_s = refs[6:]
    groups, below, share = last_shares(SLOT, last_s.shape[1])

    @pl.when(pl.program_id(0) == 0)
    def _():
        row = lax.broadcasted_iota(jnp.int32, (SLOT, SLOT), 0)
        col = lax.broadcasted_iota(jnp.int32, (SLOT, SLOT), 1)
        for prompt in range(2):
            span = slice(prompt * SLOT, (prompt + 1) * SLOT)
            first, second = parts[2 * prompt : 2 * prompt + 2]
            last_s[prompt * SLOT : prompt * SLOT + share, :] = first[:share, :]
            last_s[prompt * SLOT + share : (prompt + 1) * SLOT, :] = second[...]
            wide = 2 * HEAD_WIDTH
            sums = [first[share:, i * wide : (i + 1) * wide] for i in range(groups)]
            pair = jnp.concatenate(sums, axis=0).astype(F32)
            pair = pair + others[prompt][...].astype(F32) + own_ref[span, :].astype(F32)
            pair = pair * inv_ref[span, 0:1]
            key = rotate(pair[:, :HEAD_WIDTH], cos_ref[...], sin_ref[...])
            key_s[prompt] = key.astype(BF16)
            value_s[prompt, :, :HEAD_WIDTH] = pair[:, HEAD_WIDTH:].astype(BF16)
            value_s[prompt, :, HEAD_WIDTH:] = jnp.ones((SLOT, HEAD_WIDTH), BF16)
            seen = (col <= row) & (col < lengths_ref[prompt])
            bias_s[prompt] = jnp.where(seen, 0.0, -1e30)

    product = jnp.dot(last_s[...], w_ref[...], preferred_element_type=F32)
    row_narrow = lax.broadcasted_iota(jnp.int32, (SLOT, HEAD_WIDTH), 0)
    factor = math.log2(math.e) / math.sqrt(HEAD_WIDTH)
    for prompt, total_ref in enumerate((total_a_ref, total_b_ref)):
        rows = slice(prompt * SLOT, (prompt + 1) * SLOT)
        queries = total_ref[...] + product[rows] * inv_ref[rows, 0:1]
        for head in range(w_ref.shape[1] // HEAD_WIDTH):
            span = slice(head * HEAD_WIDTH, (head + 1) * HEAD_WIDTH)
            query = rotate(queries[:, span], cos_ref[...], sin_ref[...]).astype(BF16)
            scores = lax.dot_general(
                query, key_s[prompt], (((1,), (1,)), ((), ())), preferred_element_type=F32
            )
            scores = scores * factor + bias_s[prompt]
            top = jnp.max(scores, axis=1, keepdims=True)
            weights = jnp.exp2(scores - top)
            mixed = jnp.dot(weights.astype(BF16), value_s[prompt], preferred_element_type=F32)
            mixed = mixed[:, :HEAD_WIDTH] / mixed[:, HEAD_WIDTH:]
            mixed = jnp.where(row_narrow < lengths_ref[prompt], mixed, 0.0)
            out_ref[rows, span] = mixed.astype(BF16)


def attention(info, lengths, totals, inv, last_slot, weight, own, parts, tables):
    width = weight.shape[0] // info.shape[1]
    columns = weight.shape[1]
    tile = min(HEADS_AT_ONCE * HEAD_WIDTH, columns)
    pair = 2 * HEAD_WIDTH
    tokens = 2 * SLOT
    rows_of = [part for first, second, _ in parts for part in (first, second)]
    others = [other for _, _, other in parts]
    return call(
        attention_kernel,
        shape_of((tokens, columns), BF16),
        grid_spec=prefetch(
            2,
            (columns // tile,),
            [
                pl.BlockSpec((SLOT, tile), lambda j, *_: (0, j)),
                pl.BlockSpec((SLOT, tile), lambda j, *_: (0, j)),
                whole((tokens, LANES)),
                pl.BlockSpec((width, tile), lambda j, info, _: (info[0, last_slot], j)),
                whole((SLOT, HEAD_WIDTH)),
                whole((SLOT, HEAD_WIDTH)),
                whole((tokens, pair)),
            ]
            + [whole(part.shape) for part in rows_of]
            + [pl.BlockSpec((SLOT, pair), lambda j, *_: (0, width // pair))] * 2,
            pl.BlockSpec((tokens, tile), lambda j, *_: (0, j)),
            [
                pltpu.VMEM((tokens, width), BF16),
                pltpu.VMEM((2, SLOT, HEAD_WIDTH), BF16),
                pltpu.VMEM((2, SLOT, 2 * HEAD_WIDTH), BF16),
                pltpu.VMEM((2, SLOT, SLOT), F32),
            ],
        ),
    )(info, lengths, *totals, inv, weight, *tables, own, *rows_of, *others)


def rotation_tables():
    lane = jnp.arange(HEAD_WIDTH)
    inverse = jnp.power(F32(ROPE_BASE), -2.0 * (lane // 2).astype(F32) / HEAD_WIDTH)
    angles = jnp.arange(SLOT).astype(F32)[:, None] * inverse[None, :]
    sines = jnp.sin(angles)
    return jnp.cos(angles), jnp.where(lane[None, :] % 2 == 0, -sines, sines)


def ring_order(count):
    if count > 8:
        return list(range(count))
    return list(range(0, count, 2)) + list(range(1, count, 2))[::-1]


def after(value, *earlier):
    return lax.optimization_barrier((value, *earlier))[0]


def program(count, rows, lengths, info, x, scale, wq, wkv, wdown, wup, index, mix):
    order = ring_order(count)
    reach = count // 2
    cw = [(order[i], order[(i + 1) % count]) for i in range(count)]
    ccw = [(b, a) for a, b in cw]
    send_cw = functools.partial(lax.ppermute, axis_name="tensor", perm=cw)
    send_ccw = functools.partial(lax.ppermute, axis_name="tensor", perm=ccw)

    opposite = [(order[i], order[(i + reach) % count]) for i in range(count)]

    cw_first, ccw_first, packed = scale_rows(info, x, scale, wkv, reach)
    from_cw, from_ccw = [send_cw(cw_first), None], [send_ccw(ccw_first), None]
    low, side, cw_second, ccw_second = low_partials(
        info, x, packed, wdown, index, mix, wkv, reach
    )
    from_cw[1], from_ccw[1] = send_cw(cw_second), send_ccw(ccw_second)
    done = low
    totals = [None, None]
    inv = None
    last = []
    terms = None
    half = rows // 2

    for step in range(1, reach):
        final = step + 1 == reach
        for piece in range(2):
            got_cw, got_ccw, _ = lax.optimization_barrier((from_cw[piece], from_ccw[piece], done))
            aways = [reach - step - piece, count - reach + step + 1 - piece]
            ends = got_cw, got_ccw
            moved = list(ends)
            if final:
                sums_from, other = ends if piece == 0 else ends[::-1]
                first, second = last_messages(
                    info, sums_from, other, aways[piece], packed, wkv, terms, rows, piece
                )
                if piece == 0:
                    last.append((send_cw(first), send_ccw(second), got_ccw))
                else:
                    last.append((send_ccw(first), send_cw(second), got_cw))
                done = first
            else:
                if piece == 0:
                    moved = add_terms(info, moved, aways, packed, wkv, terms, rows)
                else:
                    moved = add_terms_low(
                        info, moved, aways, packed, wkv, terms, low, rows, step < reach - 2
                    )
                from_cw[piece], from_ccw[piece] = send_cw(moved[0]), send_ccw(moved[1])
                done = moved[piece]
            sources = [(count - step, moved[0], 0), (step, moved[1], 0)]
            if step == 1:
                sources = [(0, packed, piece * half)] + sources
            if step == 1 and piece == 1:
                opposite_low = lax.ppermute(moved[2], "tensor", opposite)
            if step == reach - 2 and piece == 1:
                late, _ = lax.optimization_barrier((opposite_low, done))
                *totals, inv = query_delta(
                    info, low, late, ends, (count - step, step), totals, wq, side, wup
                )
                done = inv
            else:
                totals[piece] = product(info, totals[piece], sources, wq, half, inv, piece)
                done = totals[piece]
            if step == 1 and piece == 0:
                *late, own = late_terms(info, after(packed, done), wkv, count)
                done = late[0]
            if step == 1 and piece == 1:
                terms = late
    return attention(info, lengths, totals, inv, reach, wq, own, last, rotation_tables())


def shards(count, x, scale, wq, wkv, wdown, wup, index, mix, lengths):
    shard = lax.axis_index("tensor")
    order = ring_order(count)
    heads = wq.shape[1] // HEAD_WIDTH
    table = np.zeros((count, 2, count), np.int32)
    for place, device in enumerate(order):
        for i in range(count):
            other = order[(place + i) % count]
            table[device, 0, i] = other
            table[device, 1, i] = other * heads // (QUERY_HEADS // KV_HEADS)
    info = lax.dynamic_index_in_dim(jnp.asarray(table), shard, 0, keepdims=False)
    return program(count, x.shape[0], lengths, info, x, scale, wq, wkv, wdown, wup, index, mix)


def solution(mesh):
    placed = (
        P(("groups", "replica"), "tensor"),
        P(),
        P(None, "tensor"),
        P("tensor", None),
        P("tensor", None),
        P(None, "tensor"),
        P(("groups", "replica"), None),
        P(("groups", "replica"), None),
        P(("groups", "replica")),
    )
    return jax.shard_map(
        functools.partial(shards, mesh.shape["tensor"]),
        mesh=mesh,
        in_specs=placed,
        out_specs=P(("groups", "replica"), "tensor"),
        check_vma=False,
    )
```
